256 devices in a mesh: row: 16 (over y_hi, x, core), col: 16 (over z, y_lo).
Axes of the slice: x: 4, y: 4 (y_hi: 2, y_lo: 2; y = y_hi * 2 + y_lo), z: 8, core: 2. Of those that a mesh axis runs over, the one named last changes fastest.
Arguments:
- inputs: bfloat16 [1024, 8192], P('col', 'row'), may hold values from -6 to 6
- gate_weight: bfloat16 [8192, 12288], P('row', 'col'), may hold values from -0.0625 to 0.0625
- up_weight: bfloat16 [8192, 12288], P('row', 'col'), may hold values from -0.0625 to 0.0625
- down_weight: bfloat16 [12288, 8192], P('col', 'row'), may hold values from -0.0546875 to 0.0546875
- out_grad: bfloat16 [1024, 8192], P('col', 'row'), may hold values from -6 to 6
Outputs:
- output: bfloat16 [1024, 8192], P('col', 'row')
- input_grad: bfloat16 [1024, 8192], P('col', 'row')
- gate_grad: bfloat16 [8192, 12288], P('row', 'col')
- up_grad: bfloat16 [8192, 12288], P('row', 'col')
- down_grad: bfloat16 [12288, 8192], P('col', 'row')
The draws below stay inside these ranges and needn't reach their ends.
All inputs are finite; a program needn't handle non-finite values.
Results may differ from the reference program's by a relative error of at most 0.005.
Values may be sent and summed in bfloat16 or wider, within the bound.
A program may use at most 64 MiB of HBM per device.

```python
import jax
import jax.numpy as jnp

D = 8192
FF = 12288
TOKENS = 1024


def strengthened(drawn, own_key, source, target, blocks, factor):
    owner, partner = [(jnp.arange(drawn.shape[position]) // (drawn.shape[position] // blocks)).reshape([-1 if axis == position else 1 for axis in range(drawn.ndim)]) for position in (source, target)]
    chosen = jax.random.permutation(own_key, blocks)[partner]
    strong = (owner == chosen) | (owner == (partner + blocks // 2) % blocks)
    return jnp.where(strong, factor * drawn, drawn)


def shard_levels(key, shape, split, smallest, top_value):
    level = 1.0
    for axis_at, parts in split:
        heights = jax.random.uniform(jax.random.fold_in(jax.random.fold_in(key, 6), axis_at), (parts,), jnp.float32, smallest / len(split), top_value / len(split))
        level = level * jnp.repeat(jnp.exp(heights), shape[axis_at] // parts).reshape((-1,) + (1,) * (len(shape) - 1 - axis_at))
    return level


def normal_values(own_key, extent, scale, bound, pieces=(), held_as=jnp.bfloat16):
    level = shard_levels(own_key, extent, pieces, -0.22, 0.18) if pieces else 1.0
    array = jax.random.normal(own_key, extent, jnp.float32) * scale * level
    return jnp.minimum(jnp.maximum(array, -bound), bound).astype(held_as)


def noise_with(own_key, shape, width, reach, split, heavy, kind=jnp.bfloat16):
    values = width * jax.random.normal(own_key, shape, jnp.float32)
    if split:
        values = values * shard_levels(own_key, shape, split, -0.22, 0.18)
    return jnp.clip(strengthened(values, jax.random.fold_in(own_key, 3), *heavy), -reach, reach).astype(kind)


def setup_inputs(seed: int = 0) -> dict:
    streams_of = jax.random.split(jax.random.key(seed), 6)
    inputs = noise_with(streams_of[0], (TOKENS, D), 1.0, 6.0, ((0, 16), (1, 16)), (1, 0, 16, 2.0))
    gate_weight = normal_values(streams_of[1], (D, FF), D ** -0.5, 0.0625, ((0, 16), (1, 16)))
    up_weight = normal_values(streams_of[2], (D, FF), D ** -0.5, 0.0625, ((0, 16), (1, 16)))
    down_weight = normal_values(streams_of[3], (FF, D), FF ** -0.5, 0.0546875, ((0, 16), (1, 16)))
    out_grad = noise_with(streams_of[4], (TOKENS, D), 1.0, 6.0, ((0, 16), (1, 16)), (1, 0, 16, 2.0))
    return dict(inputs=inputs, gate_weight=gate_weight, up_weight=up_weight, down_weight=down_weight, out_grad=out_grad)


def reference(inputs, gate_weight, up_weight, down_weight, out_grad):
    gate = jnp.dot(inputs, gate_weight, preferred_element_type=jnp.float32)
    up = jnp.dot(inputs, up_weight, preferred_element_type=jnp.float32)
    sig = jax.nn.sigmoid(gate)
    act = gate * sig
    hidden = (act * up).astype(jnp.bfloat16)
    output = jnp.dot(hidden, down_weight, preferred_element_type=jnp.float32).astype(jnp.bfloat16)
    hidden_grad = jnp.dot(out_grad, down_weight.T, preferred_element_type=jnp.float32)
    up_delta = (hidden_grad * act).astype(jnp.bfloat16)
    gate_delta = (hidden_grad * up * sig * (1.0 + gate * (1.0 - sig))).astype(jnp.bfloat16)
    input_grad = jnp.dot(gate_delta, gate_weight.T, preferred_element_type=jnp.float32)
    input_grad = input_grad + jnp.dot(up_delta, up_weight.T, preferred_element_type=jnp.float32)
    input_grad = input_grad.astype(jnp.bfloat16)
    gate_grad = jnp.dot(inputs.T, gate_delta, preferred_element_type=jnp.float32).astype(jnp.bfloat16)
    up_grad = jnp.dot(inputs.T, up_delta, preferred_element_type=jnp.float32).astype(jnp.bfloat16)
    down_grad = jnp.dot(hidden.T, out_grad, preferred_element_type=jnp.float32).astype(jnp.bfloat16)
    return output, input_grad, gate_grad, up_grad, down_grad
```

```python
import jax
import jax.numpy as jnp
from jax import lax
from jax.experimental import pallas as pl
from jax.experimental.pallas import tpu as pltpu
from jax.sharding import PartitionSpec as P

MESH = pl.DeviceIdType.MESH
F32 = jnp.float32
BF16 = jnp.bfloat16
B = 64
F = 512
H = 768
T = 256
ORDER = (4, 3, 5, 2, 6, 1, 7, 0)


def nn(left, right):
    return jnp.dot(left, right, preferred_element_type=F32)


def nt(left, right):
    return lax.dot_general(left, right, (((1,), (1,)), ((), ())), preferred_element_type=F32)


def tn(left, right):
    return lax.dot_general(left, right, (((0,), (0,)), ((), ())), preferred_element_type=F32)


def tiles(count, body):
    def step(i, carry):
        body(pl.multiple_of(i * T, T))
        return carry

    lax.fori_loop(0, count, step, 0)


class Ring:
    def __init__(self, size, pos, neighbour, partner, view, send, recv, psend, precv, pending):
        self.size, self.pos, self.neighbour, self.partner, self.view = size, pos, neighbour, partner, view
        self.sems, self.psems, self.pending = (send, recv), (psend, precv), pending

    def at(self, dist, way):
        step = 1 if way == 0 else -1
        return lax.rem(self.pos - step * dist + self.size, self.size)

    def copy(self, lane, dist, way, origin):
        ref = self.view(lane, origin)
        if 2 * dist == self.size:
            ref = ref.at[pl.ds(way * (B // 2), B // 2)]
        return pltpu.make_async_remote_copy(
            src_ref=ref,
            dst_ref=ref,
            send_sem=self.sems[0].at[way, lane, dist - 1],
            recv_sem=self.sems[1].at[way, lane, dist - 1],
            device_id=self.neighbour(way),
            device_id_type=MESH,
        )

    def send(self, lane, dist, way):
        copy = self.copy(lane, dist, way, self.at(dist - 1, way))
        copy.start()
        self.pending.append(copy)

    def wait(self, lane, dist, way):
        self.copy(lane, dist, way, self.at(dist, way)).wait_recv()

    def pair_copy(self, lane):
        ref = self.view(lane, self.pos)
        return pltpu.make_async_remote_copy(
            src_ref=ref, dst_ref=ref, send_sem=self.psems[0], recv_sem=self.psems[1],
            device_id=self.partner, device_id_type=MESH,
        )

    def send_pair(self):
        copy = self.pair_copy(0)
        copy.start()
        self.pending.append(copy)

    def wait_pair(self):
        self.pair_copy(1).wait_recv()


def kernel(
    x_hbm, wg_hbm, wu_hbm, wd_hbm, g_hbm,
    out_ref, ing_ref, gg_ref, ug_ref, dg_ref,
    xall, gall, xsib, gsib, wg, wu, wd, wgs, wus, wds,
    pg, ph, rg, rh, og, oh, acc, hall, dall, gu,
    po, pof, ro, so, zo, pi, pif, ri, si, zi, own,
    lsem, wsend, wrecv,
    xs, xr, xps, xpr, gs, gr, gps, gpr,
    xss, xsr, gss, gsr,
    rgs, rgr, rhs, rhr,
    hs, hr, hps, hpr, ds, dr, dps, dpr,
    hss, hsr, dss, dsr,
    ys, yr, zs, zr,
):
    r = lax.axis_index("row")
    c = lax.axis_index("col")
    yh, x, k = r // 8, (r // 2) % 4, r % 2
    z, yl = c // 2, c % 2
    me = yh * 4 + x
    pending = []

    sibling = (yh * 8 + x * 2 + (1 - k), c)
    yl_partner = (r, z * 2 + (1 - yl))
    yh_partner = ((1 - yh) * 8 + x * 2 + k, c)

    def z_dev(d):
        return (r, lax.rem(z + d, 8) * 2 + yl)

    def x_dev(d):
        return (yh * 8 + lax.rem(x + d, 4) * 2 + k, c)

    def row_dev(d):
        return (lax.rem(yh + d // 4, 2) * 8 + lax.rem(x + d % 4, 4) * 2 + k, c)

    def remote(src, dst, send, recv, device):
        return pltpu.make_async_remote_copy(
            src_ref=src, dst_ref=dst, send_sem=send, recv_sem=recv, device_id=device, device_id_type=MESH
        )

    def push(src, dst, send, recv, device):
        copy = remote(src, dst, send, recv, device)
        copy.start()
        pending.append(copy)

    local = [
        pltpu.make_async_copy(src, dst, lsem.at[i])
        for i, (src, dst) in enumerate((
            (x_hbm, xall.at[yl, z]), (g_hbm, gall.at[yl, z]), (wg_hbm, wg), (wu_hbm, wu), (wd_hbm, wd),
        ))
    ]
    for copy in local:
        copy.start()
    barrier = pltpu.get_barrier_semaphore()
    peers = [sibling, yl_partner] + [z_dev(d) for d in range(1, 8)] + [row_dev(d) for d in range(1, 8)]
    for peer in peers:
        pl.semaphore_signal(barrier, inc=1, device_id=peer, device_id_type=MESH)
    pl.semaphore_wait(barrier, len(peers))

    def lane_yl(lane):
        return yl if lane == 0 else 1 - yl

    def z_next(way):
        return z_dev(1 if way == 0 else 7)

    def x_next(way):
        return x_dev(1 if way == 0 else 3)

    ring_x = Ring(8, z, z_next, yl_partner, lambda lane, p: xall.at[lane_yl(lane), p], xs, xr, xps, xpr, pending)
    ring_g = Ring(8, z, z_next, yl_partner, lambda lane, p: gall.at[lane_yl(lane), p], gs, gr, gps, gpr, pending)

    def to_sibling(full, half, send, recv, p, d):
        push(full.at[1 - k, p], half.at[p], send.at[d], recv.at[d], sibling)

    def ring_start(ring):
        ring.send_pair()
        for way in (0, 1):
            ring.send(0, 1, way)

    def ring_pair(ring, full, half, send, recv):
        ring.wait_pair()
        for way in (0, 1):
            ring.send(1, 1, way)
        to_sibling(full, half, send, recv, z, 0)

    def ring_step(ring, dist, full, half, send, recv):
        for lane in (0, 1):
            for way in (0, 1):
                ring.wait(lane, dist, way)
                if dist < 4:
                    ring.send(lane, dist + 1, way)
        if dist < 4:
            for way in (0, 1):
                to_sibling(full, half, send, recv, ring.at(dist, way), dist if way == 0 else 8 - dist)
        else:
            to_sibling(full, half, send, recv, ring.at(dist, 0), dist)

    xargs = (xall, xsib, xss, xsr)
    gargs = (gall, gsib, gss, gsr)
    local[0].wait()
    ring_start(ring_x)
    local[1].wait()
    ring_start(ring_g)
    for i, (src, dst) in enumerate(((wg, wgs), (wu, wus), (wd, wds))):
        local[2 + i].wait()
        push(src, dst, wsend.at[i], wrecv.at[i], sibling)
    ring_pair(ring_x, *xargs)
    ring_step(ring_x, 1, *xargs)
    ring_pair(ring_g, *gargs)
    ring_step(ring_x, 2, *xargs)
    ring_step(ring_g, 1, *gargs)
    ring_step(ring_x, 3, *xargs)
    ring_step(ring_g, 2, *gargs)
    ring_step(ring_x, 4, *xargs)

    def wait_sibling(half, send, recv):
        for d in range(8):
            p = lax.rem(z - d + 8, 8)
            remote(half.at[p], half.at[p], send.at[d], recv.at[d], sibling).wait_recv()

    wait_sibling(xsib, xss, xsr)
    for i, dst in enumerate((wgs, wus, wds)):
        remote(dst, dst, wsend.at[i], wrecv.at[i], sibling).wait_recv()

    def put_partial(value, part, part_own, col):
        acc[...] = value
        part[:, :, pl.ds(col, T)] = value.astype(BF16).reshape(8, B, T)
        part_own[:, pl.ds(col, T)] = acc[pl.ds(pl.multiple_of(me * B, B), B), :]

    for j, (w, ws) in enumerate(((wg, wgs), (wu, wus))):
        def gate_up(col, w=w, ws=ws, j=j):
            value = nn(xall[k].reshape(8 * B, F), w[:, pl.ds(col, T)])
            value += nn(xsib[...].reshape(8 * B, F), ws[:, pl.ds(col, T)])
            put_partial(value, pg, og, pl.multiple_of(j * H + col, T))

        tiles(H // T, gate_up)

    def row_target(d):
        return lax.rem(yh + d // 4, 2) * 4 + lax.rem(x + d % 4, 4)

    for d in range(1, 8):
        push(pg.at[row_target(d)], rg.at[d - 1], rgs.at[d - 1], rgr.at[d - 1], row_dev(d))

    ring_step(ring_g, 3, *gargs)
    ring_step(ring_g, 4, *gargs)
    wait_sibling(gsib, gss, gsr)

    def hidden_grad_tile(col):
        value = nt(gall[k].reshape(8 * B, F), wd[pl.ds(col, T), :])
        value += nt(gsib[...].reshape(8 * B, F), wds[pl.ds(col, T), :])
        put_partial(value, ph, oh, col)

    tiles(H // T, hidden_grad_tile)
    for d in range(1, 8):
        push(ph.at[row_target(d)], rh.at[d - 1], rhs.at[d - 1], rhr.at[d - 1], row_dev(d))

    for d in range(1, 8):
        remote(rg.at[d - 1], rg.at[d - 1], rgs.at[d - 1], rgr.at[d - 1], row_dev(d)).wait_recv()

    def hidden_tile(col):
        up_col = pl.multiple_of(H + col, T)
        gate, up = og[:, pl.ds(col, T)], og[:, pl.ds(up_col, T)]
        for d in range(7):
            gate += rg[d, :, pl.ds(col, T)].astype(F32)
            up += rg[d, :, pl.ds(up_col, T)].astype(F32)
        gu[:, pl.ds(col, T)] = gate
        gu[:, pl.ds(up_col, T)] = up
        hall[k, me, :, pl.ds(col, T)] = (gate * jax.nn.sigmoid(gate) * up).astype(BF16)

    tiles(H // T, hidden_tile)

    def lane_slot(lane, p):
        return (yh if lane == 0 else 1 - yh) * 4 + p

    ring_h = Ring(4, x, x_next, yh_partner, lambda lane, p: hall.at[k, lane_slot(lane, p)], hs, hr, hps, hpr, pending)
    ring_d = Ring(4, x, x_next, yh_partner, lambda lane, p: dall.at[k, lane_slot(lane, p)], ds, dr, dps, dpr, pending)

    def swap(full, send, recv, lane, p, i):
        ref = full.at[k, lane_slot(lane, p)]
        push(ref, ref, send.at[i], recv.at[i], sibling)

    def row_start(ring, full, send, recv):
        ring.send_pair()
        for way in (0, 1):
            ring.send(0, 1, way)
        swap(full, send, recv, 0, x, 0)

    def row_rest(ring, full, send, recv):
        ring.wait_pair()
        for way in (0, 1):
            ring.send(1, 1, way)
        swap(full, send, recv, 1, x, 4)
        for lane in (0, 1):
            for way in (0, 1):
                ring.wait(lane, 1, way)
                ring.send(lane, 2, way)
                swap(full, send, recv, lane, ring.at(1, way), lane * 4 + 1 + 2 * way)
        for lane in (0, 1):
            for way in (0, 1):
                ring.wait(lane, 2, way)
            swap(full, send, recv, lane, ring.at(2, 0), lane * 4 + 2)

    def row_swapped(full, send, recv):
        for lane in (0, 1):
            for d in range(4):
                i = lane * 4 + d
                ref = full.at[1 - k, lane_slot(lane, lax.rem(x - d + 4, 4))]
                remote(ref, ref, send.at[i], recv.at[i], sibling).wait_recv()

    hargs = (ring_h, hall, hss, hsr)
    dargs = (ring_d, dall, dss, dsr)
    row_start(*hargs)

    for d in range(1, 8):
        remote(rh.at[d - 1], rh.at[d - 1], rhs.at[d - 1], rhr.at[d - 1], row_dev(d)).wait_recv()

    def delta_tile(col):
        up_col = pl.multiple_of(H + col, T)
        hidden_grad = oh[:, pl.ds(col, T)]
        for d in range(7):
            hidden_grad += rh[d, :, pl.ds(col, T)].astype(F32)
        gate, up = gu[:, pl.ds(col, T)], gu[:, pl.ds(up_col, T)]
        sig = jax.nn.sigmoid(gate)
        dall[k, me, :, pl.ds(up_col, T)] = (hidden_grad * (gate * sig)).astype(BF16)
        dall[k, me, :, pl.ds(col, T)] = (hidden_grad * up * sig * (1.0 + gate * (1.0 - sig))).astype(BF16)

    tiles(H // T, delta_tile)
    row_start(*dargs)
    row_rest(*hargs)
    row_swapped(hall, hss, hsr)

    def start_pair(part, received, base):
        for d in ORDER:
            p = lax.rem(z + d, 8)
            push(part.at[p], received.at[p], ys.at[base, d], yr.at[base, d], yl_partner)

    def pair_step(part_own, received, summed, landed, base, d):
        p = lax.rem(z + d, 8)
        remote(received.at[p], received.at[p], ys.at[base, d], yr.at[base, d], yl_partner).wait_recv()
        total = part_own[p] + received[p].astype(F32)
        if d == 0:
            own[base] = total
        else:
            summed[p] = total.astype(BF16)
            push(summed.at[p], landed.at[d - 1], zs.at[base, d - 1], zr.at[base, d - 1], z_dev(d))

    def finish(landed, base, result):
        for d in range(1, 8):
            remote(landed.at[d - 1], landed.at[d - 1], zs.at[base, d - 1], zr.at[base, d - 1], z_dev(d)).wait_recv()
        total = own[base]
        for d in range(7):
            total += landed[d].astype(F32)
        result[...] = total.astype(BF16)

    def out_away(col):
        po[:, :, pl.ds(col, T)] = nn(hall[1 - yl].reshape(8 * B, H), wd[:, pl.ds(col, T)]).astype(BF16).reshape(8, B, T)

    def out_home(col):
        pof[:, :, pl.ds(col, T)] = nn(hall[yl].reshape(8 * B, H), wd[:, pl.ds(col, T)]).reshape(8, B, T)

    tiles(F // T, out_away)
    start_pair(po, ro, 0)
    tiles(F // T, out_home)
    row_rest(*dargs)

    for d in ORDER:
        pair_step(pof, ro, so, zo, 0, d)

    row_swapped(dall, dss, dsr)

    def ing_tile(half, col):
        left = dall[half].reshape(8 * B, 2 * H)
        return nt(left[:, :H], wg[pl.ds(col, T), :]) + nt(left[:, H:], wu[pl.ds(col, T), :])

    def ing_away(col):
        pi[:, :, pl.ds(col, T)] = ing_tile(1 - yl, col).astype(BF16).reshape(8, B, T)

    def ing_home(col):
        pif[:, :, pl.ds(col, T)] = ing_tile(yl, col).reshape(8, B, T)

    tiles(F // T, ing_away)
    start_pair(pi, ri, 1)
    tiles(F // T, ing_home)

    def gate_grad_tile(col):
        gg_ref[:, pl.ds(col, T)] = tn(xall[...].reshape(16 * B, F), dall[:, :, :, pl.ds(col, T)].reshape(16 * B, T)).astype(BF16)

    def up_grad_tile(col):
        up_col = pl.multiple_of(H + col, T)
        ug_ref[:, pl.ds(col, T)] = tn(xall[...].reshape(16 * B, F), dall[:, :, :, pl.ds(up_col, T)].reshape(16 * B, T)).astype(BF16)

    def down_grad_tile(col):
        dg_ref[pl.ds(col, T), :] = tn(hall[:, :, :, pl.ds(col, T)].reshape(16 * B, T), gall[...].reshape(16 * B, F)).astype(BF16)

    for i, d in enumerate(ORDER):
        pair_step(pif, ri, si, zi, 1, d)
        if i == 3:
            tiles(H // T, gate_grad_tile)
    tiles(H // T, up_grad_tile)
    tiles(H // T, down_grad_tile)
    finish(zo, 0, out_ref)
    finish(zi, 1, ing_ref)
    for copy in pending:
        copy.wait_send()


def body(inputs, gate_weight, up_weight, down_weight, out_grad):
    dma = pltpu.SemaphoreType.DMA
    bf = lambda *shape: pltpu.VMEM(shape, BF16)
    f32 = lambda *shape: pltpu.VMEM(shape, F32)
    ring8 = [dma((2, 2, 4)), dma((2, 2, 4)), dma, dma]
    ring4 = [dma((2, 2, 2)), dma((2, 2, 2)), dma, dma]
    return pl.pallas_call(
        kernel,
        out_shape=(
            jax.ShapeDtypeStruct((B, F), BF16),
            jax.ShapeDtypeStruct((B, F), BF16),
            jax.ShapeDtypeStruct((F, H), BF16),
            jax.ShapeDtypeStruct((F, H), BF16),
            jax.ShapeDtypeStruct((H, F), BF16),
        ),
        in_specs=[pl.BlockSpec(memory_space=pl.ANY)] * 5,
        out_specs=(pl.BlockSpec(memory_space=pltpu.VMEM),) * 5,
        scratch_shapes=[
            bf(2, 8, B, F), bf(2, 8, B, F), bf(8, B, F), bf(8, B, F),
            bf(F, H), bf(F, H), bf(H, F), bf(F, H), bf(F, H), bf(H, F),
            bf(8, B, 2 * H), bf(8, B, H), bf(7, B, 2 * H), bf(7, B, H),
            f32(B, 2 * H), f32(B, H), f32(8 * B, T),
            bf(2, 8, B, H), bf(2, 8, B, 2 * H), f32(B, 2 * H),
            bf(8, B, F), f32(8, B, F), bf(8, B, F), bf(8, B, F), bf(7, B, F),
            bf(8, B, F), f32(8, B, F), bf(8, B, F), bf(8, B, F), bf(7, B, F),
            f32(2, B, F),
            dma((5,)), dma((3,)), dma((3,)),
            *ring8, *ring8,
            dma((8,)), dma((8,)), dma((8,)), dma((8,)),
            dma((7,)), dma((7,)), dma((7,)), dma((7,)),
            *ring4, *ring4,
            dma((8,)), dma((8,)), dma((8,)), dma((8,)),
            dma((2, 8)), dma((2, 8)), dma((2, 7)), dma((2, 7)),
        ],
        compiler_params=pltpu.CompilerParams(collective_id=0, has_side_effects=True, vmem_limit_bytes=52 << 20),
        name="ffn",
    )(inputs, gate_weight, up_weight, down_weight, out_grad)


def solution(mesh):
    return jax.shard_map(
        body,
        mesh=mesh,
        in_specs=(P("col", "row"), P("row", "col"), P("row", "col"), P("col", "row"), P("col", "row")),
        out_specs=(P("col", "row"), P("col", "row"), P("row", "col"), P("row", "col"), P("col", "row")),
        check_vma=False,
    )
```

```python
import jax
import jax.numpy as jnp
from jax import lax
from jax.experimental import pallas as pl
from jax.experimental.pallas import tpu as pltpu
from jax.sharding import PartitionSpec as P

MESH = pl.DeviceIdType.MESH
F32 = jnp.float32
BF16 = jnp.bfloat16
B = 64
F = 512
H = 768
T = 256
NEAR = (0, 1, 7, 2, 6, 3, 5, 4)
SLOT = tuple(NEAR.index(d) for d in range(8))
FAR_A = (3, 1, 2, 0)
FAR_B = (7, 5, 6, 4)
C = 4 * B
R = 32


def nn(left, right):
    return jnp.dot(left, right, preferred_element_type=F32)


def nt(left, right):
    return lax.dot_general(left, right, (((1,), (1,)), ((), ())), preferred_element_type=F32)


def tn(left, right):
    return lax.dot_general(left, right, (((0,), (0,)), ((), ())), preferred_element_type=F32)


def tiles(count, body):
    def step(i, carry):
        body(pl.multiple_of(i * T, T))
        return carry

    lax.fori_loop(0, count, step, 0)


class Ring:
    def __init__(self, far, src, dst, view, half, neighbour, sems, pending):
        self.far, self.src, self.dst, self.view, self.half = far, src, dst, view, half
        self.neighbour, self.sems, self.pending = neighbour, sems, pending

    def copy(self, src, dst, lane, dist, way):
        if dist == self.far:
            src, dst = self.half(src, way), self.half(dst, way)
        sems = [sem.at[way, lane, dist - 1] for sem in self.sems]
        return pltpu.make_async_remote_copy(
            src_ref=src, dst_ref=dst, send_sem=sems[0], recv_sem=sems[1],
            device_id=self.neighbour(way), device_id_type=MESH,
        )

    def send(self, lane, dist, way):
        copy = self.copy(self.src(lane, dist - 1, way), self.dst(lane, dist, way), lane, dist, way)
        copy.start()
        self.pending.append(copy)

    def wait(self, lane, dist, way):
        ref = self.view(lane, dist, way)
        self.copy(ref, ref, lane, dist, way).wait_recv()


def kernel(
    x_hbm, wg_hbm, wu_hbm, wd_hbm, g_hbm,
    *refs,
):
    outs = refs[:5]
    (
        xall, gall, xsib, gsib, wg, wu, wd, wgs, wus, wds, pg, ph, pgf, phf,
        glanded, gtotal, ghalf, gother, hlanded, htotal, hhalf, hother, gu, hall, dall,
        po, pof, ro, so, zo, pi, pif, ri, si, zi, own, outv, ingv, ggv, ugv, dgv,
        lsem, wsend, wrecv, xs, xr, xps, xpr, gs, gr, gps, gpr, xss, xsr, gss, gsr,
        rgs, rgr, rhs, rhr, has, har, hbs, hbr, das, dar, dbs, dbr, hss, hsr, dss, dsr, ys, yr, zs, zr, rsem,
    ) = refs[5:]
    r = lax.axis_index("row")
    c = lax.axis_index("col")
    yh, x, k = r // 8, (r // 2) % 4, r % 2
    z, yl = c // 2, c % 2
    pending = []

    sibling = (yh * 8 + x * 2 + (1 - k), c)
    yl_partner = (r, z * 2 + (1 - yl))
    yh_partner = ((1 - yh) * 8 + x * 2 + k, c)

    def z_dev(d):
        return (r, lax.rem(z + d, 8) * 2 + yl)

    def z_next(way):
        return z_dev(1 if way == 0 else 7)

    def x_dev(d):
        return (yh * 8 + lax.rem(x + d, 4) * 2 + k, c)

    def x_next(way):
        return x_dev(1 if way == 0 else 3)

    def remote(src, dst, send, recv, device):
        return pltpu.make_async_remote_copy(
            src_ref=src, dst_ref=dst, send_sem=send, recv_sem=recv, device_id=device, device_id_type=MESH
        )

    def push(src, dst, send, recv, device):
        copy = remote(src, dst, send, recv, device)
        copy.start()
        pending.append(copy)

    local = [
        pltpu.make_async_copy(src, dst, lsem.at[i])
        for i, (src, dst) in enumerate((
            (x_hbm, xall.at[yl, 0]), (g_hbm, gall.at[yl, 0]), (wg_hbm, wg), (wu_hbm, wu), (wd_hbm, wd),
        ))
    ]
    for copy in local:
        copy.start()
    barrier = pltpu.get_barrier_semaphore()
    peers = [sibling, yl_partner, yh_partner] + [x_dev(d) for d in range(1, 4)] + [z_dev(d) for d in range(1, 8)]
    for peer in peers:
        pl.semaphore_signal(barrier, inc=1, device_id=peer, device_id_type=MESH)
    pl.semaphore_wait(barrier, len(peers))

    class Gather:
        def __init__(self, full, half, sems, pair_sems, swap_sems):
            def at(lane, dist, way):
                return full.at[yl if lane == 0 else 1 - yl, SLOT[(dist if way else 8 - dist) % 8]]

            self.full, self.half_tokens, self.pair_sems, self.swap_sems = full, half, pair_sems, swap_sems
            self.ring = Ring(4, at, at, at, lambda ref, way: ref.at[pl.ds(way * R, R)], z_next, sems, pending)

        def send_pair(self):
            ref = self.full.at[yl, 0]
            push(ref, ref, *self.pair_sems, yl_partner)

        def send_own(self):
            for way in (0, 1):
                self.ring.send(0, 1, way)

        def pair(self):
            ref = self.full.at[1 - yl, 0]
            remote(ref, ref, *self.pair_sems, yl_partner).wait_recv()
            for way in (0, 1):
                self.ring.send(1, 1, way)
            self.swap(0)

        def step(self, dist):
            for lane in (0, 1):
                for way in (0, 1):
                    self.ring.wait(lane, dist, way)
                    if dist < 4:
                        self.ring.send(lane, dist + 1, way)
            for d in sorted({dist, 8 - dist}):
                self.swap(SLOT[d])

        def swap(self, s):
            send, recv = self.swap_sems
            push(self.full.at[1 - k, s], self.half_tokens.at[s], send.at[s], recv.at[s], sibling)

        def swapped(self, chunk):
            send, recv = self.swap_sems
            for s in range(4 * chunk, 4 * chunk + 4):
                ref = self.half_tokens.at[s]
                remote(ref, ref, send.at[s], recv.at[s], sibling).wait_recv()

    gat_x = Gather(xall, xsib, (xs, xr), (xps, xpr), (xss, xsr))
    gat_g = Gather(gall, gsib, (gs, gr), (gps, gpr), (gss, gsr))

    def chunk_of(ref, chunk):
        return ref[pl.ds(4 * chunk, 4)].reshape(C, F)

    def put_partial(value, part, exact, chunk, col):
        value = value.reshape(2, 4, R, T)
        exact[chunk, :, :, :, pl.ds(col, T)] = value
        part[chunk, :, :, :, pl.ds(col, T)] = value.astype(BF16)

    def gate_up_sums(chunk):
        gat_x.swapped(chunk)
        for j, (w, ws) in enumerate(((wg, wgs), (wu, wus))):
            def tile(col, w=w, ws=ws, j=j):
                value = nn(chunk_of(xall.at[k], chunk), w[:, pl.ds(col, T)])
                value += nn(chunk_of(xsib, chunk), ws[:, pl.ds(col, T)])
                put_partial(value, pg, pgf, chunk, pl.multiple_of(j * H + col, T))

            tiles(H // T, tile)

    def hidden_grad_sums(chunk):
        gat_g.swapped(chunk)

        def tile(col):
            value = nt(chunk_of(gall.at[k], chunk), wd[pl.ds(col, T), :])
            value += nt(chunk_of(gsib, chunk), wds[pl.ds(col, T), :])
            put_partial(value, ph, phf, chunk, col)

        tiles(H // T, tile)

    class RowSum:
        def __init__(self, chunk, part, exact, landed, total, half, other, sems):
            self.part, self.exact, self.landed, self.total, self.half, self.other, self.send_sem, self.recv_sem = [
                ref.at[chunk] for ref in (part, exact, landed, total, half, other, *sems)
            ]

        def send(self):
            for d in (2, 1, 3):
                src = self.part.at[:, lax.rem(x + d, 4)]
                push(src, self.landed.at[d - 1], self.send_sem.at[d - 1], self.recv_sem.at[d - 1], x_dev(d))

        def arrived(self, ref, i):
            remote(ref, ref, self.send_sem.at[i], self.recv_sem.at[i], yh_partner).wait_recv()

        def pair(self):
            for d in range(3):
                self.arrived(self.landed.at[d], d)
            for lane in (0, 1):
                value = self.exact[lane, x]
                for d in range(3):
                    value += self.landed[d, lane].astype(F32)
                self.total[lane] = value
                self.half[lane] = value.astype(BF16)
            push(self.half, self.other, self.send_sem.at[3], self.recv_sem.at[3], yh_partner)

        def finish(self):
            self.arrived(self.other, 3)

        def value(self, lane, col):
            return self.total[lane, :, pl.ds(col, T)] + self.other[lane, :, pl.ds(col, T)].astype(F32)

    sum_gu = [RowSum(i, pg, pgf, glanded, gtotal, ghalf, gother, (rgs, rgr)) for i in (0, 1)]
    sum_h = [RowSum(i, ph, phf, hlanded, htotal, hhalf, hother, (rhs, rhr)) for i in (0, 1)]

    def hidden_of(chunk):
        sum_gu[chunk].finish()

        def tile(col):
            up_col = pl.multiple_of(H + col, T)
            for lane in (0, 1):
                gate, up = sum_gu[chunk].value(lane, col), sum_gu[chunk].value(lane, up_col)
                gu[chunk, lane, :, pl.ds(col, T)] = gate
                gu[chunk, lane, :, pl.ds(up_col, T)] = up
                hall[k, chunk, lane, x, :, pl.ds(col, T)] = (gate * jax.nn.sigmoid(gate) * up).astype(BF16)

        tiles(H // T, tile)

    def deltas_of(chunk):
        sum_h[chunk].finish()

        def tile(col):
            up_col = pl.multiple_of(H + col, T)
            for lane in (0, 1):
                hidden_grad = sum_h[chunk].value(lane, col)
                gate, up = gu[chunk, lane, :, pl.ds(col, T)], gu[chunk, lane, :, pl.ds(up_col, T)]
                sig = jax.nn.sigmoid(gate)
                dall[k, chunk, lane, x, :, pl.ds(up_col, T)] = (hidden_grad * (gate * sig)).astype(BF16)
                dall[k, chunk, lane, x, :, pl.ds(col, T)] = (
                    hidden_grad * up * sig * (1.0 + gate * (1.0 - sig))
                ).astype(BF16)

        tiles(H // T, tile)

    class RowGather:
        def __init__(self, full, chunk, sems, swap_sems):
            self.full, self.chunk, self.swap_sems = full, chunk, [sem.at[chunk] for sem in swap_sems]

            def src(lane, dist, way):
                return self.block(k, dist if way else 4 - dist)

            def dst(lane, dist, way):
                return src(lane, dist - 1, way)

            self.ring = Ring(2, src, dst, src, lambda ref, way: ref.at[way], x_next, sems, pending)

        def block(self, core, d):
            return self.full.at[core, self.chunk, :, lax.rem(x + d, 4)]

        def swap(self, d):
            ref = self.block(k, d)
            push(ref, ref, self.swap_sems[0].at[d], self.swap_sems[1].at[d], sibling)

        def start(self):
            for way in (0, 1):
                self.ring.send(0, 1, way)
            self.swap(0)

        def near(self):
            for way in (0, 1):
                self.ring.wait(0, 1, way)
                self.ring.send(0, 2, way)
                self.swap(1 if way else 3)

        def far(self):
            for way in (0, 1):
                self.ring.wait(0, 2, way)
            self.swap(2)

        def swapped(self):
            for d in range(4):
                ref = self.block(1 - k, d)
                remote(ref, ref, self.swap_sems[0].at[d], self.swap_sems[1].at[d], sibling).wait_recv()

    hid_a = RowGather(hall, 0, (has, har), (hss, hsr))
    hid_b = RowGather(hall, 1, (hbs, hbr), (hss, hsr))
    del_a = RowGather(dall, 0, (das, dar), (dss, dsr))
    del_b = RowGather(dall, 1, (dbs, dbr), (dss, dsr))

    class ColSum:
        def __init__(self, base, part, exact, received, summed, landed, result):
            self.base, self.part, self.exact, self.received = base, part, exact, received
            self.summed, self.landed, self.result = summed, landed, result

        def start(self, slots):
            for s in slots:
                push(self.part.at[s], self.received.at[s], ys.at[self.base, s], yr.at[self.base, s], yl_partner)

        def step(self, s):
            ref, d = self.received.at[s], NEAR[s]
            remote(ref, ref, ys.at[self.base, s], yr.at[self.base, s], yl_partner).wait_recv()
            total = self.exact[s] + self.received[s].astype(F32)
            if d == 0:
                own[self.base] = total
            else:
                self.summed[s] = total.astype(BF16)
                push(self.summed.at[s], self.landed.at[d - 1], zs.at[self.base, d - 1], zr.at[self.base, d - 1], z_dev(d))

        def finish(self):
            total = own[self.base]
            for d in (1, 7, 2, 6, 3, 5, 4):
                ref = self.landed.at[d - 1]
                remote(ref, ref, zs.at[self.base, d - 1], zr.at[self.base, d - 1], z_dev(d)).wait_recv()
            for d in range(7):
                total += self.landed[d].astype(F32)
            self.result[...] = total.astype(BF16)

    sum_out = ColSum(0, po, pof, ro, so, zo, outv)
    sum_ing = ColSum(1, pi, pif, ri, si, zi, ingv)

    def out_tile(half, chunk, col):
        return nn(hall[half, chunk].reshape(C, H), wd[:, pl.ds(col, T)])

    def ing_tile(half, chunk, col):
        left = dall[half, chunk].reshape(C, 2 * H)
        return nt(left[:, :H], wg[pl.ds(col, T), :]) + nt(left[:, H:], wu[pl.ds(col, T), :])

    def col_sums(total, tile, chunk, slots):
        def away(col):
            total.part[pl.ds(4 * chunk, 4), :, pl.ds(col, T)] = tile(1 - yl, chunk, col).astype(BF16).reshape(4, B, T)

        def home(col):
            total.exact[pl.ds(4 * chunk, 4), :, pl.ds(col, T)] = tile(yl, chunk, col).reshape(4, B, T)

        tiles(F // T, away)
        total.start(slots)
        tiles(F // T, home)

    def tokens(ref, col):
        return ref[:, :, :, :, :, pl.ds(col, T)].reshape(16 * B, T)

    def gate_grad_tile(col):
        ggv[:, pl.ds(col, T)] = tn(xall[...].reshape(16 * B, F), tokens(dall, col)).astype(BF16)

    def up_grad_tile(col):
        up_col = pl.multiple_of(H + col, T)
        ugv[:, pl.ds(col, T)] = tn(xall[...].reshape(16 * B, F), tokens(dall, up_col)).astype(BF16)

    def down_grad_tile(col):
        dgv[pl.ds(col, T), :] = tn(tokens(hall, col), gall[...].reshape(16 * B, F)).astype(BF16)

    results = [
        pltpu.make_async_copy(src, dst, rsem.at[i]) for i, (src, dst) in enumerate(zip((outv, ingv, ggv, ugv, dgv), outs))
    ]

    local[0].wait()
    gat_x.send_pair()
    gat_x.send_own()
    local[1].wait()
    gat_g.send_pair()
    for i, (src, dst) in enumerate(((wg, wgs), (wu, wus), (wd, wds))):
        local[2 + i].wait()
        push(src, dst, wsend.at[i], wrecv.at[i], sibling)
    gat_x.pair()
    gat_x.step(1)
    gat_g.send_own()
    gat_x.step(2)
    for i, dst in enumerate((wgs, wus, wds)):
        remote(dst, dst, wsend.at[i], wrecv.at[i], sibling).wait_recv()
    gat_g.pair()
    gate_up_sums(0)
    sum_gu[0].send()
    gat_x.step(3)
    gat_g.step(1)
    gat_x.step(4)
    gat_g.step(2)
    gate_up_sums(1)
    sum_gu[1].send()
    gat_g.step(3)
    sum_gu[0].pair()
    hidden_grad_sums(0)
    sum_h[0].send()
    gat_g.step(4)
    hidden_grad_sums(1)
    sum_h[1].send()
    hidden_of(0)
    hid_a.start()
    sum_gu[1].pair()
    sum_h[0].pair()
    hidden_of(1)
    hid_b.start()
    sum_h[1].pair()
    deltas_of(0)
    del_a.start()
    hid_a.near()
    deltas_of(1)
    del_b.start()
    hid_b.near()
    hid_a.far()
    del_a.near()
    hid_a.swapped()
    col_sums(sum_out, out_tile, 0, FAR_A)
    hid_b.far()
    del_b.near()
    hid_b.swapped()
    col_sums(sum_out, out_tile, 1, FAR_B)
    for s in FAR_A:
        sum_out.step(s)
    del_a.far()
    del_a.swapped()
    col_sums(sum_ing, ing_tile, 0, FAR_A)
    for s in FAR_B:
        sum_out.step(s)
    del_b.far()
    del_b.swapped()
    col_sums(sum_ing, ing_tile, 1, FAR_B)
    tiles(H // T, down_grad_tile)
    results[4].start()
    for s in FAR_A:
        sum_ing.step(s)
    tiles(H // T, gate_grad_tile)
    results[2].start()
    for s in FAR_B:
        sum_ing.step(s)
    tiles(H // T, up_grad_tile)
    results[3].start()
    sum_out.finish()
    results[0].start()
    sum_ing.finish()
    results[1].start()
    for copy in pending:
        copy.wait_send()
    for copy in results:
        copy.wait()


def deliver(*refs):
    sources, results, held, sems = refs[:5], refs[5:10], refs[10:15], refs[15]
    loads = [pltpu.make_async_copy(sources[i], held[i], sems.at[0, i]) for i in range(5)]
    stores = [pltpu.make_async_copy(held[i], results[i], sems.at[1, i]) for i in range(5)]
    for load in loads:
        load.start()
    for load, store in zip(loads, stores):
        load.wait()
        store.start()
    for store in stores:
        store.wait()


def body(inputs, gate_weight, up_weight, down_weight, out_grad):
    dma = pltpu.SemaphoreType.DMA
    shapes = tuple(jax.ShapeDtypeStruct(shape, BF16) for shape in ((B, F), (B, F), (F, H), (F, H), (H, F)))
    bf = lambda *shape: pltpu.VMEM(shape, BF16)
    f32 = lambda *shape: pltpu.VMEM(shape, F32)
    ring = lambda lanes, far: [dma((2, lanes, far))] * 2
    results = pl.pallas_call(
        kernel,
        out_shape=shapes,
        in_specs=[pl.BlockSpec(memory_space=pl.ANY)] * 5,
        out_specs=(pl.BlockSpec(memory_space=pl.ANY),) * 5,
        scratch_shapes=[
            bf(2, 8, B, F), bf(2, 8, B, F), bf(8, B, F), bf(8, B, F),
            bf(F, H), bf(F, H), bf(H, F), bf(F, H), bf(F, H), bf(H, F),
            bf(2, 2, 4, R, 2 * H), bf(2, 2, 4, R, H), f32(2, 2, 4, R, 2 * H), f32(2, 2, 4, R, H),
            bf(2, 3, 2, R, 2 * H), f32(2, 2, R, 2 * H), bf(2, 2, R, 2 * H), bf(2, 2, R, 2 * H),
            bf(2, 3, 2, R, H), f32(2, 2, R, H), bf(2, 2, R, H), bf(2, 2, R, H),
            f32(2, 2, R, 2 * H), bf(2, 2, 2, 4, R, H), bf(2, 2, 2, 4, R, 2 * H),
            bf(8, B, F), f32(8, B, F), bf(8, B, F), bf(8, B, F), bf(7, B, F),
            bf(8, B, F), f32(8, B, F), bf(8, B, F), bf(8, B, F), bf(7, B, F),
            f32(2, B, F), bf(B, F), bf(B, F), bf(F, H), bf(F, H), bf(H, F),
            dma((5,)), dma((3,)), dma((3,)),
            *ring(2, 4), dma, dma, *ring(2, 4), dma, dma,
            dma((8,)), dma((8,)), dma((8,)), dma((8,)),
            dma((2, 4)), dma((2, 4)), dma((2, 4)), dma((2, 4)),
            *ring(1, 2), *ring(1, 2), *ring(1, 2), *ring(1, 2),
            dma((2, 4)), dma((2, 4)), dma((2, 4)), dma((2, 4)),
            dma((2, 8)), dma((2, 8)), dma((2, 7)), dma((2, 7)), dma((5,)),
        ],
        compiler_params=pltpu.CompilerParams(collective_id=0, has_side_effects=True, vmem_limit_bytes=60 << 20),
        name="ffn",
    )(inputs, gate_weight, up_weight, down_weight, out_grad)
    return pl.pallas_call(
        deliver,
        out_shape=shapes,
        in_specs=[pl.BlockSpec(memory_space=pl.ANY)] * 5,
        out_specs=(pl.BlockSpec(memory_space=pl.ANY),) * 5,
        scratch_shapes=[*[pltpu.VMEM(shape.shape, BF16) for shape in shapes], dma((2, 5))],
        name="deliver",
    )(*results)


def solution(mesh):
    return jax.shard_map(
        body,
        mesh=mesh,
        in_specs=(P("col", "row"), P("row", "col"), P("row", "col"), P("col", "row"), P("col", "row")),
        out_specs=(P("col", "row"), P("col", "row"), P("row", "col"), P("row", "col"), P("col", "row")),
        check_vma=False,
    )
```

```python
import jax
import jax.numpy as jnp
from jax import lax
from jax.experimental import pallas as pl
from jax.experimental.pallas import tpu as pltpu
from jax.sharding import PartitionSpec as P

MESH = pl.DeviceIdType.MESH
F32 = jnp.float32
BF16 = jnp.bfloat16
B = 64
F = 512
H = 768
T = 256
NEAR = (0, 1, 7, 2, 6, 3, 5, 4)
SLOT = tuple(NEAR.index(d) for d in range(8))
N = 4
S = 8 // N
C = S * B
R = C // 8
POOL = 48


def nn(left, right):
    return jnp.dot(left, right, preferred_element_type=F32)


def nt(left, right):
    return lax.dot_general(left, right, (((1,), (1,)), ((), ())), preferred_element_type=F32)


def tn(left, right):
    return lax.dot_general(left, right, (((0,), (0,)), ((), ())), preferred_element_type=F32)


def tiles(count, body):
    def step(i, carry):
        body(pl.multiple_of(i * T, T))
        return carry

    lax.fori_loop(0, count, step, 0)


class Ring:
    def __init__(self, far, src, dst, view, half, neighbour, sems, push, wait_for):
        self.far, self.src, self.dst, self.view, self.half = far, src, dst, view, half
        self.neighbour, self.sems, self.push, self.wait_for = neighbour, sems, push, wait_for

    def part(self, ref, dist, way):
        return self.half(ref, way) if dist == self.far else ref

    def send(self, lane, dist, way):
        src, dst = [self.part(ref, dist, way) for ref in (self.src(lane, dist - 1, way), self.dst(lane, dist, way))]
        self.push(src, dst, self.sems.at[way, lane, dist - 1], self.neighbour(way))

    def wait(self, lane, dist, way):
        self.wait_for(self.part(self.view(lane, dist, way), dist, way), self.sems.at[way, lane, dist - 1])


def kernel(
    x_hbm, wg_hbm, wu_hbm, wd_hbm, g_hbm,
    *refs,
):
    outs = refs[:5]
    (
        xall, gall, xsib, gsib, wg, wu, wd, wgs, wus, wds, pg, ph, pgf, phf,
        glanded, gtotal, ghalf, gother, hlanded, htotal, hhalf, hother, gu, hall, dall,
        po, pof, ro, so, zo, pi, pif, ri, si, zi, own, outv, ingv, ggv, ugv, dgv,
        lsem, pool, wrecv, xr, xpr, gr, gpr, xsr, gsr, rgr, rhr, hr, dr, hsr, dsr, yr, zr, rsem,
    ) = refs[5:]
    r = lax.axis_index("row")
    c = lax.axis_index("col")
    yh, x, k = r // 8, (r // 2) % 4, r % 2
    z, yl = c // 2, c % 2
    pending = []

    sibling = (yh * 8 + x * 2 + (1 - k), c)
    yl_partner = (r, z * 2 + (1 - yl))
    yh_partner = ((1 - yh) * 8 + x * 2 + k, c)

    def z_dev(d):
        return (r, lax.rem(z + d, 8) * 2 + yl)

    def z_next(way):
        return z_dev(1 if way == 0 else 7)

    def x_dev(d):
        return (yh * 8 + lax.rem(x + d, 4) * 2 + k, c)

    def x_next(way):
        return x_dev(1 if way == 0 else 3)

    def push(src, dst, recv, device):
        count = len(pending)
        if count >= POOL:
            pending[count - POOL].wait_send()
        copy = pltpu.make_async_remote_copy(
            src_ref=src, dst_ref=dst, send_sem=pool.at[count % POOL], recv_sem=recv,
            device_id=device, device_id_type=MESH,
        )
        copy.start()
        pending.append(copy)

    def wait_for(ref, recv):
        pltpu.make_async_remote_copy(
            src_ref=ref, dst_ref=ref, send_sem=pool.at[0], recv_sem=recv, device_id=sibling, device_id_type=MESH
        ).wait_recv()

    local = [
        pltpu.make_async_copy(src, dst, lsem.at[i])
        for i, (src, dst) in enumerate((
            (x_hbm, xall.at[yl, 0]), (g_hbm, gall.at[yl, 0]), (wg_hbm, wg), (wu_hbm, wu), (wd_hbm, wd),
        ))
    ]
    for copy in local:
        copy.start()
    barrier = pltpu.get_barrier_semaphore()
    peers = [sibling, yl_partner, yh_partner] + [x_dev(d) for d in range(1, 4)] + [z_dev(d) for d in range(1, 8)]
    for peer in peers:
        pl.semaphore_signal(barrier, inc=1, device_id=peer, device_id_type=MESH)
    pl.semaphore_wait(barrier, len(peers))

    def half_rows(ref, way):
        return ref.at[pl.ds(way * (B // 2), B // 2)]

    class Gather:
        def __init__(self, full, half, recv, pair_recv, swap_recv):
            def at(lane, dist, way):
                return full.at[yl if lane == 0 else 1 - yl, SLOT[(dist if way else 8 - dist) % 8]]

            self.full, self.half_tokens, self.pair_recv, self.swap_recv = full, half, pair_recv, swap_recv
            self.ring = Ring(4, at, at, at, half_rows, z_next, recv, push, wait_for)

        def send_pair(self):
            ref = self.full.at[yl, 0]
            push(ref, ref, self.pair_recv, yl_partner)

        def send_own(self):
            for way in (0, 1):
                self.ring.send(0, 1, way)

        def pair(self):
            ref = self.full.at[1 - yl, 0]
            wait_for(ref, self.pair_recv)
            for way in (0, 1):
                self.ring.send(1, 1, way)
            self.swap(0)

        def step(self, dist):
            for lane in (0, 1):
                for way in (0, 1):
                    self.ring.wait(lane, dist, way)
                    if dist < 4:
                        self.ring.send(lane, dist + 1, way)
            for d in sorted({dist, 8 - dist}):
                self.swap(SLOT[d])

        def swap(self, s):
            push(self.full.at[1 - k, s], self.half_tokens.at[s], self.swap_recv.at[s // S], sibling)

        def swapped(self, chunk):
            wait_for(self.half_tokens.at[pl.ds(S * chunk, S)], self.swap_recv.at[chunk])

    gat_x = Gather(xall, xsib, xr, xpr, xsr)
    gat_g = Gather(gall, gsib, gr, gpr, gsr)

    def chunk_of(ref, chunk):
        return ref[pl.ds(S * chunk, S)].reshape(C, F)

    def put_partial(value, part, exact, chunk, col):
        value = value.reshape(2, 4, R, T)
        exact[chunk, :, :, :, pl.ds(col, T)] = value
        part[chunk, :, :, :, pl.ds(col, T)] = value.astype(BF16)

    def gate_up_sums(chunk):
        gat_x.swapped(chunk)
        for j, (w, ws) in enumerate(((wg, wgs), (wu, wus))):
            def tile(col, w=w, ws=ws, j=j):
                value = nn(chunk_of(xall.at[k], chunk), w[:, pl.ds(col, T)])
                value += nn(chunk_of(xsib, chunk), ws[:, pl.ds(col, T)])
                put_partial(value, pg, pgf, chunk, pl.multiple_of(j * H + col, T))

            tiles(H // T, tile)

    def hidden_grad_sums(chunk):
        gat_g.swapped(chunk)

        def tile(col):
            value = nt(chunk_of(gall.at[k], chunk), wd[pl.ds(col, T), :])
            value += nt(chunk_of(gsib, chunk), wds[pl.ds(col, T), :])
            put_partial(value, ph, phf, chunk, col)

        tiles(H // T, tile)

    class RowSum:
        def __init__(self, chunk, part, exact, landed, total, half, other, recv):
            self.part, self.exact, self.landed, self.total, self.half, self.other, self.recv = [
                ref.at[chunk] for ref in (part, exact, landed, total, half, other, recv)
            ]

        def send(self):
            for d in (2, 1, 3):
                src = self.part.at[:, lax.rem(x + d, 4)]
                push(src, self.landed.at[d - 1], self.recv.at[0], x_dev(d))

        def pair(self):
            wait_for(self.landed, self.recv.at[0])
            for lane in (0, 1):
                value = self.exact[lane, x]
                for d in range(3):
                    value += self.landed[d, lane].astype(F32)
                self.total[lane] = value
                self.half[lane] = value.astype(BF16)
            push(self.half, self.other, self.recv.at[1], yh_partner)

        def finish(self):
            wait_for(self.other, self.recv.at[1])

        def value(self, lane, col):
            return self.total[lane, :, pl.ds(col, T)] + self.other[lane, :, pl.ds(col, T)].astype(F32)

    sum_gu = [RowSum(i, pg, pgf, glanded, gtotal, ghalf, gother, rgr) for i in range(N)]
    sum_h = [RowSum(i, ph, phf, hlanded, htotal, hhalf, hother, rhr) for i in range(N)]

    def gate_up(chunk):
        gate_up_sums(chunk)
        sum_gu[chunk].send()

    def hidden_grad(chunk):
        hidden_grad_sums(chunk)
        sum_h[chunk].send()

    def hidden_of(chunk):
        sum_gu[chunk].finish()

        def tile(col):
            up_col = pl.multiple_of(H + col, T)
            for lane in (0, 1):
                gate, up = sum_gu[chunk].value(lane, col), sum_gu[chunk].value(lane, up_col)
                gu[chunk, lane, :, pl.ds(col, T)] = gate
                gu[chunk, lane, :, pl.ds(up_col, T)] = up
                hall[k, chunk, lane, x, :, pl.ds(col, T)] = (gate * jax.nn.sigmoid(gate) * up).astype(BF16)

        tiles(H // T, tile)
        hid[chunk].start()

    def deltas_of(chunk):
        sum_h[chunk].finish()

        def tile(col):
            up_col = pl.multiple_of(H + col, T)
            for lane in (0, 1):
                hidden_grad = sum_h[chunk].value(lane, col)
                gate, up = gu[chunk, lane, :, pl.ds(col, T)], gu[chunk, lane, :, pl.ds(up_col, T)]
                sig = jax.nn.sigmoid(gate)
                dall[k, chunk, lane, x, :, pl.ds(up_col, T)] = (hidden_grad * (gate * sig)).astype(BF16)
                dall[k, chunk, lane, x, :, pl.ds(col, T)] = (
                    hidden_grad * up * sig * (1.0 + gate * (1.0 - sig))
                ).astype(BF16)

        tiles(H // T, tile)
        delta[chunk].start()

    class RowGather:
        def __init__(self, full, chunk, recv, swap_recv, straight):
            self.full, self.chunk, self.straight = full, chunk, straight
            self.far_recv, self.swap_recv = recv.at[0, 0, 1], swap_recv.at[chunk]

            def src(lane, dist, way):
                return self.block(k, dist if way else 4 - dist)

            def dst(lane, dist, way):
                return src(lane, dist - 1, way)

            self.ring = Ring(2, src, dst, src, lambda ref, way: ref.at[way], x_next, recv, push, wait_for)

        def block(self, core, d):
            return self.full.at[core, self.chunk, :, lax.rem(x + d, 4)]

        def swap(self, d):
            ref = self.block(k, d)
            push(ref, ref, self.swap_recv, sibling)

        def start(self):
            for way in (0, 1):
                self.ring.send(0, 1, way)
            if self.straight:
                push(self.block(k, 0), self.block(k, 0), self.far_recv, x_dev(2))
            self.swap(0)

        def near(self):
            for way in (0, 1):
                self.ring.wait(0, 1, way)
                if not self.straight:
                    self.ring.send(0, 2, way)
                self.swap(1 if way else 3)

        def far(self):
            if self.straight:
                wait_for(self.block(k, 2), self.far_recv)
            else:
                for way in (0, 1):
                    self.ring.wait(0, 2, way)
            self.swap(2)

        def swapped(self):
            wait_for(self.full.at[1 - k, self.chunk], self.swap_recv)

    hid = [RowGather(hall, i, hr.at[i], hsr, True) for i in range(N)]
    delta = [RowGather(dall, i, dr.at[i], dsr, False) for i in range(N)]

    class ColSum:
        def __init__(self, base, part, exact, received, summed, landed, result):
            self.base, self.part, self.exact, self.received = base, part, exact, received
            self.summed, self.landed, self.result = summed, landed, result

        def start(self, chunk):
            for s in reversed(range(S * chunk, S * chunk + S)):
                push(self.part.at[1 - yl, s], self.received.at[s], yr.at[self.base, s], yl_partner)

        def steps(self, chunk):
            for s in reversed(range(S * chunk, S * chunk + S)):
                self.step(s)

        def step(self, s):
            d = NEAR[s]
            wait_for(self.received.at[s], yr.at[self.base, s])
            total = self.exact[yl, s] + self.received[s].astype(F32)
            if d == 0:
                own[self.base] = total
            else:
                self.summed[s] = total.astype(BF16)
                push(self.summed.at[s], self.landed.at[d - 1], zr.at[self.base], z_dev(d))

        def finish(self):
            total = own[self.base]
            wait_for(self.landed, zr.at[self.base])
            for d in range(7):
                total += self.landed[d].astype(F32)
            self.result[...] = total.astype(BF16)

    sum_out = ColSum(0, po, pof, ro, so, zo, outv)
    sum_ing = ColSum(1, pi, pif, ri, si, zi, ingv)

    def out_tile(chunk, col):
        return nn(hall[:, chunk].reshape(2 * C, H), wd[:, pl.ds(col, T)])

    def ing_tile(chunk, col):
        left = dall[:, chunk].reshape(2 * C, 2 * H)
        return nt(left[:, :H], wg[pl.ds(col, T), :]) + nt(left[:, H:], wu[pl.ds(col, T), :])

    def col_sums(total, tile, chunk):
        slots = pl.ds(S * chunk, S)

        def both(col):
            value = tile(chunk, col).reshape(2, S, B, T)
            total.exact[:, slots, :, pl.ds(col, T)] = value
            total.part[:, slots, :, pl.ds(col, T)] = value.astype(BF16)

        tiles(F // T, both)
        total.start(chunk)

    def out_sums(chunk):
        hid[chunk].swapped()
        col_sums(sum_out, out_tile, chunk)

    def ing_sums(chunk):
        delta[chunk].swapped()
        col_sums(sum_ing, ing_tile, chunk)

    def tokens(ref, col):
        return ref[:, :, :, :, :, pl.ds(col, T)].reshape(16 * B, T)

    def gate_grad_tile(col):
        ggv[:, pl.ds(col, T)] = tn(xall[...].reshape(16 * B, F), tokens(dall, col)).astype(BF16)

    def up_grad_tile(col):
        up_col = pl.multiple_of(H + col, T)
        ugv[:, pl.ds(col, T)] = tn(xall[...].reshape(16 * B, F), tokens(dall, up_col)).astype(BF16)

    def down_grad_tile(col):
        dgv[pl.ds(col, T), :] = tn(tokens(hall, col), gall[...].reshape(16 * B, F)).astype(BF16)

    results = [
        pltpu.make_async_copy(src, dst, rsem.at[i]) for i, (src, dst) in enumerate(zip((outv, ingv, ggv, ugv, dgv), outs))
    ]

    local[0].wait()
    gat_x.send_pair()
    gat_x.send_own()
    local[1].wait()
    gat_g.send_pair()
    for i, (src, dst) in enumerate(((wg, wgs), (wu, wus), (wd, wds))):
        local[2 + i].wait()
        push(src, dst, wrecv.at[i], sibling)
    gat_x.pair()
    gat_x.step(1)
    gat_g.send_own()
    for i, dst in enumerate((wgs, wus, wds)):
        wait_for(dst, wrecv.at[i])
    gate_up(0)
    gat_x.step(2)
    gat_g.pair()
    gate_up(1)
    gat_x.step(3)
    gat_g.step(1)
    sum_gu[0].pair()
    gate_up(2)
    gat_x.step(4)
    gat_g.step(2)
    sum_gu[1].pair()
    hidden_of(0)
    gate_up(3)
    gat_g.step(3)
    sum_gu[2].pair()
    hidden_of(1)
    gat_g.step(4)
    hidden_grad(3)
    hid[0].near()
    hid[0].far()
    hidden_of(2)
    hidden_grad(2)
    sum_gu[3].pair()
    hidden_grad(1)
    sum_h[3].pair()
    out_sums(0)
    hid[1].near()
    hid[1].far()
    hidden_of(3)
    hidden_grad(0)
    sum_h[2].pair()
    deltas_of(3)
    out_sums(1)
    hid[2].near()
    hid[2].far()
    sum_out.steps(0)
    sum_h[1].pair()
    deltas_of(2)
    out_sums(2)
    hid[3].near()
    hid[3].far()
    sum_h[0].pair()
    sum_out.steps(1)
    out_sums(3)
    delta[3].near()
    deltas_of(1)
    sum_out.steps(2)
    delta[2].near()
    deltas_of(0)
    sum_out.steps(3)
    delta[3].far()
    delta[1].near()
    ing_sums(3)
    delta[2].far()
    delta[0].near()
    ing_sums(2)
    sum_ing.steps(3)
    delta[1].far()
    delta[0].far()
    ing_sums(1)
    ing_sums(0)
    sum_ing.steps(2)
    tiles(H // T, down_grad_tile)
    results[4].start()
    sum_ing.steps(1)
    tiles(H // T, gate_grad_tile)
    results[2].start()
    sum_ing.steps(0)
    tiles(H // T, up_grad_tile)
    results[3].start()
    sum_out.finish()
    results[0].start()
    sum_ing.finish()
    results[1].start()
    for copy in pending[-POOL:]:
        copy.wait_send()
    for copy in results:
        copy.wait()


def deliver(*refs):
    sources, results, held, sems = refs[:5], refs[5:10], refs[10:15], refs[15]
    loads = [pltpu.make_async_copy(sources[i], held[i], sems.at[0, i]) for i in range(5)]
    stores = [pltpu.make_async_copy(held[i], results[i], sems.at[1, i]) for i in range(5)]
    for load in loads:
        load.start()
    for load, store in zip(loads, stores):
        load.wait()
        store.start()
    for store in stores:
        store.wait()


def body(inputs, gate_weight, up_weight, down_weight, out_grad):
    dma = pltpu.SemaphoreType.DMA
    shapes = tuple(jax.ShapeDtypeStruct(shape, BF16) for shape in ((B, F), (B, F), (F, H), (F, H), (H, F)))
    bf = lambda *shape: pltpu.VMEM(shape, BF16)
    f32 = lambda *shape: pltpu.VMEM(shape, F32)
    results = pl.pallas_call(
        kernel,
        out_shape=shapes,
        in_specs=[pl.BlockSpec(memory_space=pl.ANY)] * 5,
        out_specs=(pl.BlockSpec(memory_space=pl.ANY),) * 5,
        scratch_shapes=[
            bf(2, 8, B, F), bf(2, 8, B, F), bf(8, B, F), bf(8, B, F),
            bf(F, H), bf(F, H), bf(H, F), bf(F, H), bf(F, H), bf(H, F),
            bf(N, 2, 4, R, 2 * H), bf(N, 2, 4, R, H), f32(N, 2, 4, R, 2 * H), f32(N, 2, 4, R, H),
            bf(N, 3, 2, R, 2 * H), f32(N, 2, R, 2 * H), bf(N, 2, R, 2 * H), bf(N, 2, R, 2 * H),
            bf(N, 3, 2, R, H), f32(N, 2, R, H), bf(N, 2, R, H), bf(N, 2, R, H),
            f32(N, 2, R, 2 * H), bf(2, N, 2, 4, R, H), bf(2, N, 2, 4, R, 2 * H),
            bf(2, 8, B, F), f32(2, 8, B, F), bf(8, B, F), bf(8, B, F), bf(7, B, F),
            bf(2, 8, B, F), f32(2, 8, B, F), bf(8, B, F), bf(8, B, F), bf(7, B, F),
            f32(2, B, F), bf(B, F), bf(B, F), bf(F, H), bf(F, H), bf(H, F),
            dma((5,)), dma((POOL,)), dma((3,)),
            dma((2, 2, 4)), dma, dma((2, 2, 4)), dma, dma((N,)), dma((N,)),
            dma((N, 2)), dma((N, 2)), dma((N, 2, 1, 2)), dma((N, 2, 1, 2)), dma((N,)), dma((N,)),
            dma((2, 8)), dma((2,)), dma((5,)),
        ],
        compiler_params=pltpu.CompilerParams(collective_id=0, has_side_effects=True, vmem_limit_bytes=60 << 20),
        name="ffn",
    )(inputs, gate_weight, up_weight, down_weight, out_grad)
    return pl.pallas_call(
        deliver,
        out_shape=shapes,
        in_specs=[pl.BlockSpec(memory_space=pl.ANY)] * 5,
        out_specs=(pl.BlockSpec(memory_space=pl.ANY),) * 5,
        scratch_shapes=[*[pltpu.VMEM(shape.shape, BF16) for shape in shapes], dma((2, 5))],
        name="deliver",
    )(*results)


def solution(mesh):
    return jax.shard_map(
        body,
        mesh=mesh,
        in_specs=(P("col", "row"), P("row", "col"), P("row", "col"), P("col", "row"), P("col", "row")),
        out_specs=(P("col", "row"), P("col", "row"), P("row", "col"), P("row", "col"), P("col", "row")),
        check_vma=False,
    )
```

```python
import jax
import jax.numpy as jnp
from jax import lax
from jax.experimental import pallas as pl
from jax.experimental.pallas import tpu as pltpu
from jax.sharding import PartitionSpec as P

MESH = pl.DeviceIdType.MESH
F32 = jnp.float32
BF16 = jnp.bfloat16
B = 64
F = 512
H = 768
T = 256
NEAR = (0, 1, 7, 2, 6, 3, 5, 4)
SLOT = tuple(NEAR.index(d) for d in range(8))
N = 4
S = 8 // N
C = S * B
R = C // 8
POOL = 48
HID_STRAIGHT = (False, False, False, True)
DELTA_STRAIGHT = (True, False, True, True)


def nn(left, right):
    return jnp.dot(left, right, preferred_element_type=F32)


def nt(left, right):
    return lax.dot_general(left, right, (((1,), (1,)), ((), ())), preferred_element_type=F32)


def tn(left, right):
    return lax.dot_general(left, right, (((0,), (0,)), ((), ())), preferred_element_type=F32)


def tiles(count, body):
    def step(i, carry):
        body(pl.multiple_of(i * T, T))
        return carry

    lax.fori_loop(0, count, step, 0)


class Ring:
    def __init__(self, far, src, dst, view, half, neighbour, sems, push, wait_for):
        self.far, self.src, self.dst, self.view, self.half = far, src, dst, view, half
        self.neighbour, self.sems, self.push, self.wait_for = neighbour, sems, push, wait_for

    def part(self, ref, dist, way):
        return self.half(ref, way) if dist == self.far else ref

    def send(self, lane, dist, way):
        src, dst = [self.part(ref, dist, way) for ref in (self.src(lane, dist - 1, way), self.dst(lane, dist, way))]
        self.push(src, dst, self.sems.at[way, lane, dist - 1], self.neighbour(way))

    def wait(self, lane, dist, way):
        self.wait_for(self.part(self.view(lane, dist, way), dist, way), self.sems.at[way, lane, dist - 1])


def kernel(
    x_hbm, wg_hbm, wu_hbm, wd_hbm, g_hbm,
    *refs,
):
    outs = refs[:5]
    (
        xall, gall, xsib, gsib, wg, wu, wd, wgs, wus, wds, pg, ph, pgf, phf,
        glanded, gtotal, ghalf, gother, hlanded, htotal, hhalf, hother, gu, hall, dall,
        po, pof, ro, so, zo, pi, pif, ri, si, zi, own, outv, ingv, ggv, ugv, dgv,
        lsem, pool, wrecv, xr, xpr, gr, gpr, xsr, gsr, rgr, rhr, hr, dr, hsr, dsr, yr, zr, rsem,
    ) = refs[5:]
    r = lax.axis_index("row")
    c = lax.axis_index("col")
    yh, x, k = r // 8, (r // 2) % 4, r % 2
    z, yl = c // 2, c % 2
    pending = []

    sibling = (yh * 8 + x * 2 + (1 - k), c)
    yl_partner = (r, z * 2 + (1 - yl))
    yh_partner = ((1 - yh) * 8 + x * 2 + k, c)

    def z_dev(d):
        return (r, lax.rem(z + d, 8) * 2 + yl)

    def z_next(way):
        return z_dev(1 if way == 0 else 7)

    def x_dev(d):
        return (yh * 8 + lax.rem(x + d, 4) * 2 + k, c)

    def x_next(way):
        return x_dev(1 if way == 0 else 3)

    def push(src, dst, recv, device):
        count = len(pending)
        if count >= POOL:
            pending[count - POOL].wait_send()
        copy = pltpu.make_async_remote_copy(
            src_ref=src, dst_ref=dst, send_sem=pool.at[count % POOL], recv_sem=recv,
            device_id=device, device_id_type=MESH,
        )
        copy.start()
        pending.append(copy)

    def wait_for(ref, recv):
        pltpu.make_async_remote_copy(
            src_ref=ref, dst_ref=ref, send_sem=pool.at[0], recv_sem=recv, device_id=sibling, device_id_type=MESH
        ).wait_recv()

    local = [
        pltpu.make_async_copy(src, dst, lsem.at[i])
        for i, (src, dst) in enumerate((
            (x_hbm, xall.at[yl, 0]), (g_hbm, gall.at[yl, 0]), (wg_hbm, wg), (wu_hbm, wu), (wd_hbm, wd),
        ))
    ]
    for copy in local:
        copy.start()
    barrier = pltpu.get_barrier_semaphore()
    peers = [sibling, yl_partner, yh_partner] + [x_dev(d) for d in range(1, 4)] + [z_dev(d) for d in range(1, 8)]
    for peer in peers:
        pl.semaphore_signal(barrier, inc=1, device_id=peer, device_id_type=MESH)
    pl.semaphore_wait(barrier, len(peers))

    def half_rows(ref, way):
        return ref.at[pl.ds(way * (B // 2), B // 2)]

    class Gather:
        def __init__(self, full, half, recv, pair_recv, swap_recv):
            def at(lane, dist, way):
                return full.at[yl if lane == 0 else 1 - yl, SLOT[(dist if way else 8 - dist) % 8]]

            self.full, self.half_tokens, self.pair_recv, self.swap_recv = full, half, pair_recv, swap_recv
            self.ring = Ring(4, at, at, at, half_rows, z_next, recv, push, wait_for)

        def send_pair(self):
            ref = self.full.at[yl, 0]
            push(ref, ref, self.pair_recv, yl_partner)

        def send_own(self):
            for way in (0, 1):
                self.ring.send(0, 1, way)

        def pair(self):
            ref = self.full.at[1 - yl, 0]
            wait_for(ref, self.pair_recv)
            for way in (0, 1):
                self.ring.send(1, 1, way)
            self.swap(0)

        def step(self, dist):
            for lane in (0, 1):
                for way in (0, 1):
                    self.ring.wait(lane, dist, way)
                    if dist < 4:
                        self.ring.send(lane, dist + 1, way)
            for d in sorted({dist, 8 - dist}):
                self.swap(SLOT[d])

        def swap(self, s):
            push(self.full.at[1 - k, s], self.half_tokens.at[s], self.swap_recv.at[s // S], sibling)

        def swapped(self, chunk):
            wait_for(self.half_tokens.at[pl.ds(S * chunk, S)], self.swap_recv.at[chunk])

    gat_x = Gather(xall, xsib, xr, xpr, xsr)
    gat_g = Gather(gall, gsib, gr, gpr, gsr)

    def chunk_of(ref, chunk):
        return ref[pl.ds(S * chunk, S)].reshape(C, F)

    def put_partial(value, part, exact, chunk, col):
        value = value.reshape(2, 4, R, T)
        exact[chunk, :, :, :, pl.ds(col, T)] = value
        part[chunk, :, :, :, pl.ds(col, T)] = value.astype(BF16)

    def half_sums(chunk, j):
        w, ws = ((wg, wgs), (wu, wus))[j]

        def tile(col):
            value = nn(chunk_of(xall.at[k], chunk), w[:, pl.ds(col, T)])
            value += nn(chunk_of(xsib, chunk), ws[:, pl.ds(col, T)])
            put_partial(value, pg, pgf, chunk, pl.multiple_of(j * H + col, T))

        tiles(H // T, tile)

    def hidden_grad_sums(chunk):
        gat_g.swapped(chunk)

        def tile(col):
            value = nt(chunk_of(gall.at[k], chunk), wd[pl.ds(col, T), :])
            value += nt(chunk_of(gsib, chunk), wds[pl.ds(col, T), :])
            put_partial(value, ph, phf, chunk, col)

        tiles(H // T, tile)

    class RowSum:
        def __init__(self, chunk, part, exact, landed, total, half, other, recv):
            self.part, self.exact, self.landed, self.total, self.half, self.other, self.recv = [
                ref.at[chunk] for ref in (part, exact, landed, total, half, other, recv)
            ]

        def send(self, first):
            cols = pl.ds(first, H)
            for d in (2, 1, 3):
                src = self.part.at[:, lax.rem(x + d, 4), :, cols]
                push(src, self.landed.at[d - 1, :, :, cols], self.recv.at[0], x_dev(d))

        def pair(self):
            wait_for(self.landed, self.recv.at[0])
            for lane in (0, 1):
                value = self.exact[lane, x]
                for d in range(3):
                    value += self.landed[d, lane].astype(F32)
                self.total[lane] = value
                self.half[lane] = value.astype(BF16)
            push(self.half, self.other, self.recv.at[1], yh_partner)

        def finish(self):
            wait_for(self.other, self.recv.at[1])

        def value(self, lane, col):
            return self.total[lane, :, pl.ds(col, T)] + self.other[lane, :, pl.ds(col, T)].astype(F32)

    sum_gu = [RowSum(i, pg, pgf, glanded, gtotal, ghalf, gother, rgr) for i in range(N)]
    sum_h = [RowSum(i, ph, phf, hlanded, htotal, hhalf, hother, rhr) for i in range(N)]

    def gate_part(chunk):
        gat_x.swapped(chunk)
        half_sums(chunk, 0)
        sum_gu[chunk].send(0)

    def up_part(chunk):
        half_sums(chunk, 1)
        sum_gu[chunk].send(H)

    def hidden_grad(chunk):
        hidden_grad_sums(chunk)
        sum_h[chunk].send(0)

    def hidden_of(chunk):
        sum_gu[chunk].finish()

        def tile(col):
            up_col = pl.multiple_of(H + col, T)
            for lane in (0, 1):
                gate, up = sum_gu[chunk].value(lane, col), sum_gu[chunk].value(lane, up_col)
                gu[chunk, lane, :, pl.ds(col, T)] = gate
                gu[chunk, lane, :, pl.ds(up_col, T)] = up
                hall[k, chunk, lane, x, :, pl.ds(col, T)] = (gate * jax.nn.sigmoid(gate) * up).astype(BF16)

        tiles(H // T, tile)
        hid[chunk].start()

    def deltas_of(chunk):
        sum_h[chunk].finish()

        def tile(col):
            up_col = pl.multiple_of(H + col, T)
            for lane in (0, 1):
                hidden_grad = sum_h[chunk].value(lane, col)
                gate, up = gu[chunk, lane, :, pl.ds(col, T)], gu[chunk, lane, :, pl.ds(up_col, T)]
                sig = jax.nn.sigmoid(gate)
                dall[k, chunk, lane, x, :, pl.ds(up_col, T)] = (hidden_grad * (gate * sig)).astype(BF16)
                dall[k, chunk, lane, x, :, pl.ds(col, T)] = (
                    hidden_grad * up * sig * (1.0 + gate * (1.0 - sig))
                ).astype(BF16)

        tiles(H // T, tile)
        delta[chunk].start()

    class RowGather:
        def __init__(self, full, chunk, recv, swap_recv, straight):
            self.full, self.chunk, self.straight = full, chunk, straight
            self.far_recv, self.swap_recv = recv.at[0, 0, 1], swap_recv.at[chunk]

            def src(lane, dist, way):
                return self.block(k, dist if way else 4 - dist)

            def dst(lane, dist, way):
                return src(lane, dist - 1, way)

            self.ring = Ring(2, src, dst, src, lambda ref, way: ref.at[way], x_next, recv, push, wait_for)

        def block(self, core, d):
            return self.full.at[core, self.chunk, :, lax.rem(x + d, 4)]

        def swap(self, d):
            ref = self.block(k, d)
            push(ref, ref, self.swap_recv, sibling)

        def start(self):
            for way in (0, 1):
                self.ring.send(0, 1, way)
            if self.straight:
                push(self.block(k, 0), self.block(k, 0), self.far_recv, x_dev(2))
            self.swap(0)

        def near(self):
            for way in (0, 1):
                self.ring.wait(0, 1, way)
                if not self.straight:
                    self.ring.send(0, 2, way)
                self.swap(1 if way else 3)

        def far(self):
            if self.straight:
                wait_for(self.block(k, 2), self.far_recv)
            else:
                for way in (0, 1):
                    self.ring.wait(0, 2, way)
            self.swap(2)

        def swapped(self):
            wait_for(self.full.at[1 - k, self.chunk], self.swap_recv)

    hid = [RowGather(hall, i, hr.at[i], hsr, HID_STRAIGHT[i]) for i in range(N)]
    delta = [RowGather(dall, i, dr.at[i], dsr, DELTA_STRAIGHT[i]) for i in range(N)]

    class ColSum:
        def __init__(self, base, part, exact, received, summed, landed, result):
            self.base, self.part, self.exact, self.received = base, part, exact, received
            self.summed, self.landed, self.result = summed, landed, result

        def start(self, chunk):
            for s in reversed(range(S * chunk, S * chunk + S)):
                push(self.part.at[1 - yl, s], self.received.at[s], yr.at[self.base, s], yl_partner)

        def steps(self, chunk):
            for s in reversed(range(S * chunk, S * chunk + S)):
                self.step(s)

        def step(self, s):
            d = NEAR[s]
            wait_for(self.received.at[s], yr.at[self.base, s])
            total = self.exact[yl, s] + self.received[s].astype(F32)
            if d == 0:
                own[self.base] = total
            else:
                self.summed[s] = total.astype(BF16)
                push(self.summed.at[s], self.landed.at[d - 1], zr.at[self.base], z_dev(d))

        def finish(self):
            total = own[self.base]
            wait_for(self.landed, zr.at[self.base])
            for d in range(7):
                total += self.landed[d].astype(F32)
            self.result[...] = total.astype(BF16)

    sum_out = ColSum(0, po, pof, ro, so, zo, outv)
    sum_ing = ColSum(1, pi, pif, ri, si, zi, ingv)

    def out_tile(chunk, col):
        return nn(hall[:, chunk].reshape(2 * C, H), wd[:, pl.ds(col, T)])

    def ing_tile(chunk, col):
        left = dall[:, chunk].reshape(2 * C, 2 * H)
        return nt(left[:, :H], wg[pl.ds(col, T), :]) + nt(left[:, H:], wu[pl.ds(col, T), :])

    def col_sums(total, tile, chunk):
        slots = pl.ds(S * chunk, S)

        def both(col):
            value = tile(chunk, col).reshape(2, S, B, T)
            total.exact[:, slots, :, pl.ds(col, T)] = value
            total.part[:, slots, :, pl.ds(col, T)] = value.astype(BF16)

        tiles(F // T, both)
        total.start(chunk)

    def out_sums(chunk):
        hid[chunk].swapped()
        col_sums(sum_out, out_tile, chunk)

    def ing_sums(chunk):
        delta[chunk].swapped()
        col_sums(sum_ing, ing_tile, chunk)

    def tokens(ref, col):
        return ref[:, :, :, :, :, pl.ds(col, T)].reshape(16 * B, T)

    def gate_grad_tile(col):
        ggv[:, pl.ds(col, T)] = tn(xall[...].reshape(16 * B, F), tokens(dall, col)).astype(BF16)

    def up_grad_tile(col):
        up_col = pl.multiple_of(H + col, T)
        ugv[:, pl.ds(col, T)] = tn(xall[...].reshape(16 * B, F), tokens(dall, up_col)).astype(BF16)

    def down_grad_tile(col):
        dgv[pl.ds(col, T), :] = tn(tokens(hall, col), gall[...].reshape(16 * B, F)).astype(BF16)

    results = [
        pltpu.make_async_copy(src, dst, rsem.at[i]) for i, (src, dst) in enumerate(zip((outv, ingv, ggv, ugv, dgv), outs))
    ]

    local[0].wait()
    gat_x.send_pair()
    gat_x.send_own()
    local[1].wait()
    gat_g.send_pair()
    for i, (src, dst) in enumerate(((wg, wgs), (wu, wus), (wd, wds))):
        local[2 + i].wait()
        push(src, dst, wrecv.at[i], sibling)
    gat_x.pair()
    gat_g.send_own()
    gat_x.step(1)
    gat_g.pair()
    for i, dst in enumerate((wgs, wus, wds)):
        wait_for(dst, wrecv.at[i])
    gate_part(0)
    up_part(0)
    gat_x.step(2)
    gate_part(1)
    up_part(1)
    gat_g.step(1)
    gat_x.step(3)
    gate_part(2)
    up_part(2)
    gat_g.step(2)
    sum_gu[1].pair()
    sum_gu[0].pair()
    gat_x.step(4)
    gate_part(3)
    up_part(3)
    hidden_of(1)
    sum_gu[2].pair()
    hidden_grad(1)
    gat_g.step(3)
    hidden_grad(2)
    sum_gu[3].pair()
    hid[1].near()
    gat_g.step(4)
    hidden_of(2)
    hidden_of(3)
    hidden_grad(3)
    hid[1].far()
    hidden_of(0)
    sum_h[1].pair()
    hid[2].near()
    sum_h[2].pair()
    out_sums(1)
    hid[3].near()
    hid[3].far()
    deltas_of(1)
    sum_h[3].pair()
    out_sums(3)
    hid[0].near()
    hidden_grad(0)
    sum_out.step(3)
    sum_out.step(2)
    hid[2].far()
    out_sums(2)
    delta[1].near()
    hid[0].far()
    sum_out.step(7)
    deltas_of(3)
    sum_out.step(6)
    out_sums(0)
    delta[1].far()
    sum_h[0].pair()
    sum_out.step(5)
    ing_sums(1)
    deltas_of(2)
    sum_out.step(1)
    delta[3].near()
    sum_out.step(4)
    delta[3].far()
    ing_sums(3)
    deltas_of(0)
    sum_out.step(0)
    delta[2].near()
    sum_ing.step(3)
    sum_ing.step(2)
    delta[2].far()
    sum_ing.step(7)
    ing_sums(2)
    delta[0].near()
    sum_ing.step(6)
    tiles(H // T, down_grad_tile)
    results[4].start()
    delta[0].far()
    sum_ing.step(5)
    ing_sums(0)
    sum_ing.step(4)
    sum_out.finish()
    results[0].start()
    tiles(H // T, up_grad_tile)
    results[3].start()
    sum_ing.step(1)
    tiles(H // T, gate_grad_tile)
    results[2].start()
    sum_ing.step(0)
    sum_ing.finish()
    results[1].start()
    for copy in pending[-POOL:]:
        copy.wait_send()
    for copy in results:
        copy.wait()


def deliver(*refs):
    sources, results, held, sems = refs[:5], refs[5:10], refs[10:15], refs[15]
    pieces = [(i, pl.ds(row, 128)) for i in range(2, 5) for row in range(0, sources[i].shape[0], 128)]
    pieces += [(i, pl.ds(0, B)) for i in range(2)]
    loads = [pltpu.make_async_copy(sources[i].at[r], held[i].at[r], sems.at[0, n]) for n, (i, r) in enumerate(pieces)]
    stores = [pltpu.make_async_copy(held[i].at[r], results[i].at[r], sems.at[1, n]) for n, (i, r) in enumerate(pieces)]
    for load in loads:
        load.start()
    for load, store in zip(loads, stores):
        load.wait()
        store.start()
    for store in stores:
        store.wait()


def body(inputs, gate_weight, up_weight, down_weight, out_grad):
    dma = pltpu.SemaphoreType.DMA
    shapes = tuple(jax.ShapeDtypeStruct(shape, BF16) for shape in ((B, F), (B, F), (F, H), (F, H), (H, F)))
    bf = lambda *shape: pltpu.VMEM(shape, BF16)
    f32 = lambda *shape: pltpu.VMEM(shape, F32)
    results = pl.pallas_call(
        kernel,
        out_shape=shapes,
        in_specs=[pl.BlockSpec(memory_space=pl.ANY)] * 5,
        out_specs=(pl.BlockSpec(memory_space=pl.ANY),) * 5,
        scratch_shapes=[
            bf(2, 8, B, F), bf(2, 8, B, F), bf(8, B, F), bf(8, B, F),
            bf(F, H), bf(F, H), bf(H, F), bf(F, H), bf(F, H), bf(H, F),
            bf(N, 2, 4, R, 2 * H), bf(N, 2, 4, R, H), f32(N, 2, 4, R, 2 * H), f32(N, 2, 4, R, H),
            bf(N, 3, 2, R, 2 * H), f32(N, 2, R, 2 * H), bf(N, 2, R, 2 * H), bf(N, 2, R, 2 * H),
            bf(N, 3, 2, R, H), f32(N, 2, R, H), bf(N, 2, R, H), bf(N, 2, R, H),
            f32(N, 2, R, 2 * H), bf(2, N, 2, 4, R, H), bf(2, N, 2, 4, R, 2 * H),
            bf(2, 8, B, F), f32(2, 8, B, F), bf(8, B, F), bf(8, B, F), bf(7, B, F),
            bf(2, 8, B, F), f32(2, 8, B, F), bf(8, B, F), bf(8, B, F), bf(7, B, F),
            f32(2, B, F), bf(B, F), bf(B, F), bf(F, H), bf(F, H), bf(H, F),
            dma((5,)), dma((POOL,)), dma((3,)),
            dma((2, 2, 4)), dma, dma((2, 2, 4)), dma, dma((N,)), dma((N,)),
            dma((N, 2)), dma((N, 2)), dma((N, 2, 1, 2)), dma((N, 2, 1, 2)), dma((N,)), dma((N,)),
            dma((2, 8)), dma((2,)), dma((5,)),
        ],
        compiler_params=pltpu.CompilerParams(collective_id=0, has_side_effects=True, vmem_limit_bytes=60 << 20),
        name="ffn",
    )(inputs, gate_weight, up_weight, down_weight, out_grad)
    return pl.pallas_call(
        deliver,
        out_shape=shapes,
        in_specs=[pl.BlockSpec(memory_space=pl.ANY)] * 5,
        out_specs=(pl.BlockSpec(memory_space=pl.ANY),) * 5,
        scratch_shapes=[*[pltpu.VMEM(shape.shape, BF16) for shape in shapes], dma((2, 16))],
        name="deliver",
    )(*results)


def solution(mesh):
    return jax.shard_map(
        body,
        mesh=mesh,
        in_specs=(P("col", "row"), P("row", "col"), P("row", "col"), P("col", "row"), P("col", "row")),
        out_specs=(P("col", "row"), P("col", "row"), P("row", "col"), P("row", "col"), P("col", "row")),
        check_vma=False,
    )
```

```python
import jax
import jax.numpy as jnp
from jax import lax
from jax.experimental import pallas as pl
from jax.experimental.pallas import tpu as pltpu
from jax.sharding import PartitionSpec as P

MESH = pl.DeviceIdType.MESH
F32 = jnp.float32
BF16 = jnp.bfloat16
B = 64
F = 512
H = 768
T = 256
NEAR = (0, 1, 7, 2, 6, 3, 5, 4)
SLOT = tuple(NEAR.index(d) for d in range(8))
N = 4
S = 8 // N
C = S * B
R = C // 8
POOL = 48
HID_STRAIGHT = (False, False, False, True)
DELTA_STRAIGHT = (True, False, True, True)


def nn(left, right):
    return jnp.dot(left, right, preferred_element_type=F32)


def nt(left, right):
    return lax.dot_general(left, right, (((1,), (1,)), ((), ())), preferred_element_type=F32)


def tn(left, right):
    return lax.dot_general(left, right, (((0,), (0,)), ((), ())), preferred_element_type=F32)


def tiles(count, body):
    def step(i, carry):
        body(pl.multiple_of(i * T, T))
        return carry

    lax.fori_loop(0, count, step, 0)


class Ring:
    def __init__(self, far, src, dst, view, half, neighbour, sems, push, wait_for):
        self.far, self.src, self.dst, self.view, self.half = far, src, dst, view, half
        self.neighbour, self.sems, self.push, self.wait_for = neighbour, sems, push, wait_for

    def part(self, ref, dist, way):
        return self.half(ref, way) if dist == self.far else ref

    def send(self, lane, dist, way):
        src, dst = [self.part(ref, dist, way) for ref in (self.src(lane, dist - 1, way), self.dst(lane, dist, way))]
        self.push(src, dst, self.sems.at[way, lane, dist - 1], self.neighbour(way))

    def wait(self, lane, dist, way):
        self.wait_for(self.part(self.view(lane, dist, way), dist, way), self.sems.at[way, lane, dist - 1])


def kernel(
    x_hbm, wg_hbm, wu_hbm, wd_hbm, g_hbm,
    *refs,
):
    outs = refs[:5]
    (
        xall, gall, xsib, gsib, wg, wu, wd, wgs, wus, wds, pg, ph, pgf, phf,
        glanded, gtotal, ghalf, gother, hlanded, htotal, hhalf, hother, gu, hall, dall,
        po, pof, ro, so, zo, pi, pif, ri, si, zi, own, outv, ingv, ggv, ugv, dgv,
        lsem, pool, wrecv, xr, xpr, gr, gpr, xsr, gsr, rgr, rhr, hr, dr, hsr, dsr, yr, zr, rsem,
    ) = refs[5:]
    r = lax.axis_index("row")
    c = lax.axis_index("col")
    yh, x, k = r // 8, (r // 2) % 4, r % 2
    z, yl = c // 2, c % 2
    pending = []

    sibling = (yh * 8 + x * 2 + (1 - k), c)
    yl_partner = (r, z * 2 + (1 - yl))
    yh_partner = ((1 - yh) * 8 + x * 2 + k, c)

    def z_dev(d):
        return (r, lax.rem(z + d, 8) * 2 + yl)

    def z_next(way):
        return z_dev(1 if way == 0 else 7)

    def x_dev(d):
        return (yh * 8 + lax.rem(x + d, 4) * 2 + k, c)

    def x_next(way):
        return x_dev(1 if way == 0 else 3)

    def push(src, dst, recv, device):
        count = len(pending)
        if count >= POOL:
            pending[count - POOL].wait_send()
        copy = pltpu.make_async_remote_copy(
            src_ref=src, dst_ref=dst, send_sem=pool.at[count % POOL], recv_sem=recv,
            device_id=device, device_id_type=MESH,
        )
        copy.start()
        pending.append(copy)

    def wait_for(ref, recv):
        pltpu.make_async_remote_copy(
            src_ref=ref, dst_ref=ref, send_sem=pool.at[0], recv_sem=recv, device_id=sibling, device_id_type=MESH
        ).wait_recv()

    local = [
        pltpu.make_async_copy(src, dst, lsem.at[i])
        for i, (src, dst) in enumerate((
            (x_hbm, xall.at[yl, 0]), (g_hbm, gall.at[yl, 0]), (wg_hbm, wg), (wu_hbm, wu), (wd_hbm, wd),
        ))
    ]
    for copy in local:
        copy.start()
    barrier = pltpu.get_barrier_semaphore()
    peers = [sibling, yl_partner, yh_partner] + [x_dev(d) for d in range(1, 4)] + [z_dev(d) for d in range(1, 8)]
    for peer in peers:
        pl.semaphore_signal(barrier, inc=1, device_id=peer, device_id_type=MESH)
    pl.semaphore_wait(barrier, len(peers))

    def half_rows(ref, way):
        return ref.at[pl.ds(way * (B // 2), B // 2)]

    class Gather:
        def __init__(self, full, half, recv, pair_recv, swap_recv):
            def at(lane, dist, way):
                return full.at[yl if lane == 0 else 1 - yl, SLOT[(dist if way else 8 - dist) % 8]]

            self.full, self.half_tokens, self.pair_recv, self.swap_recv = full, half, pair_recv, swap_recv
            self.ring = Ring(4, at, at, at, half_rows, z_next, recv, push, wait_for)

        def send_pair(self):
            ref = self.full.at[yl, 0]
            push(ref, ref, self.pair_recv, yl_partner)

        def send_own(self):
            for way in (0, 1):
                self.ring.send(0, 1, way)

        def pair(self):
            ref = self.full.at[1 - yl, 0]
            wait_for(ref, self.pair_recv)
            for way in (0, 1):
                self.ring.send(1, 1, way)
            self.swap(0)

        def step(self, dist):
            for lane in (0, 1):
                for way in (0, 1):
                    self.ring.wait(lane, dist, way)
                    if dist < 4:
                        self.ring.send(lane, dist + 1, way)
            for d in sorted({dist, 8 - dist}):
                self.swap(SLOT[d])

        def swap(self, s):
            push(self.full.at[1 - k, s], self.half_tokens.at[s], self.swap_recv.at[s // S], sibling)

        def swapped(self, chunk):
            wait_for(self.half_tokens.at[pl.ds(S * chunk, S)], self.swap_recv.at[chunk])

    gat_x = Gather(xall, xsib, xr, xpr, xsr)
    gat_g = Gather(gall, gsib, gr, gpr, gsr)

    def chunk_of(ref, chunk):
        return ref[pl.ds(S * chunk, S)].reshape(C, F)

    def put_partial(value, part, exact, chunk, col):
        value = value.reshape(2, 4, R, T)
        exact[chunk, :, :, :, pl.ds(col, T)] = value
        part[chunk, :, :, :, pl.ds(col, T)] = value.astype(BF16)

    def half_sums(chunk, j):
        w, ws = ((wg, wgs), (wu, wus))[j]

        def tile(col):
            value = nn(chunk_of(xall.at[k], chunk), w[:, pl.ds(col, T)])
            value += nn(chunk_of(xsib, chunk), ws[:, pl.ds(col, T)])
            put_partial(value, pg, pgf, chunk, pl.multiple_of(j * H + col, T))

        tiles(H // T, tile)

    def hidden_grad_sums(chunk):
        gat_g.swapped(chunk)

        def tile(col):
            value = nt(chunk_of(gall.at[k], chunk), wd[pl.ds(col, T), :])
            value += nt(chunk_of(gsib, chunk), wds[pl.ds(col, T), :])
            put_partial(value, ph, phf, chunk, col)

        tiles(H // T, tile)

    class RowSum:
        def __init__(self, chunk, part, exact, landed, total, half, other, recv):
            self.part, self.exact, self.landed, self.total, self.half, self.other, self.recv = [
                ref.at[chunk] for ref in (part, exact, landed, total, half, other, recv)
            ]

        def send(self, first):
            cols = pl.ds(first, H)
            for d in (2, 1, 3):
                src = self.part.at[:, lax.rem(x + d, 4), :, cols]
                push(src, self.landed.at[d - 1, :, :, cols], self.recv.at[0], x_dev(d))

        def pair(self):
            wait_for(self.landed, self.recv.at[0])
            for lane in (0, 1):
                value = self.exact[lane, x]
                for d in range(3):
                    value += self.landed[d, lane].astype(F32)
                self.total[lane] = value
                self.half[lane] = value.astype(BF16)
            push(self.half, self.other, self.recv.at[1], yh_partner)

        def finish(self):
            wait_for(self.other, self.recv.at[1])

        def value(self, lane, col):
            return self.total[lane, :, pl.ds(col, T)] + self.other[lane, :, pl.ds(col, T)].astype(F32)

    sum_gu = [RowSum(i, pg, pgf, glanded, gtotal, ghalf, gother, rgr) for i in range(N)]
    sum_h = [RowSum(i, ph, phf, hlanded, htotal, hhalf, hother, rhr) for i in range(N)]

    def gate_part(chunk):
        gat_x.swapped(chunk)
        half_sums(chunk, 0)
        sum_gu[chunk].send(0)

    def up_part(chunk):
        half_sums(chunk, 1)
        sum_gu[chunk].send(H)

    def hidden_grad(chunk):
        hidden_grad_sums(chunk)
        sum_h[chunk].send(0)

    def hidden_of(chunk):
        sum_gu[chunk].finish()

        def tile(col):
            up_col = pl.multiple_of(H + col, T)
            for lane in (0, 1):
                gate, up = sum_gu[chunk].value(lane, col), sum_gu[chunk].value(lane, up_col)
                gu[chunk, lane, :, pl.ds(col, T)] = gate
                gu[chunk, lane, :, pl.ds(up_col, T)] = up
                hall[k, chunk, lane, x, :, pl.ds(col, T)] = (gate * jax.nn.sigmoid(gate) * up).astype(BF16)

        tiles(H // T, tile)
        hid[chunk].start()

    def deltas_of(chunk):
        sum_h[chunk].finish()

        def tile(col):
            up_col = pl.multiple_of(H + col, T)
            for lane in (0, 1):
                hidden_grad = sum_h[chunk].value(lane, col)
                gate, up = gu[chunk, lane, :, pl.ds(col, T)], gu[chunk, lane, :, pl.ds(up_col, T)]
                sig = jax.nn.sigmoid(gate)
                dall[k, chunk, lane, x, :, pl.ds(up_col, T)] = (hidden_grad * (gate * sig)).astype(BF16)
                dall[k, chunk, lane, x, :, pl.ds(col, T)] = (
                    hidden_grad * up * sig * (1.0 + gate * (1.0 - sig))
                ).astype(BF16)

        tiles(H // T, tile)
        delta[chunk].start()

    class RowGather:
        def __init__(self, full, chunk, recv, swap_recv, straight):
            self.full, self.chunk, self.straight = full, chunk, straight
            self.far_recv, self.swap_recv = recv.at[0, 0, 1], swap_recv.at[chunk]

            def src(lane, dist, way):
                return self.block(k, dist if way else 4 - dist)

            def dst(lane, dist, way):
                return src(lane, dist - 1, way)

            self.ring = Ring(2, src, dst, src, lambda ref, way: ref.at[way], x_next, recv, push, wait_for)

        def block(self, core, d):
            return self.full.at[core, self.chunk, :, lax.rem(x + d, 4)]

        def swap(self, d):
            ref = self.block(k, d)
            push(ref, ref, self.swap_recv, sibling)

        def start(self):
            for way in (0, 1):
                self.ring.send(0, 1, way)
            if self.straight:
                push(self.block(k, 0), self.block(k, 0), self.far_recv, x_dev(2))
            self.swap(0)

        def near(self):
            for way in (0, 1):
                self.ring.wait(0, 1, way)
                if not self.straight:
                    self.ring.send(0, 2, way)
                self.swap(1 if way else 3)

        def far(self):
            if self.straight:
                wait_for(self.block(k, 2), self.far_recv)
            else:
                for way in (0, 1):
                    self.ring.wait(0, 2, way)
            self.swap(2)

        def swapped(self):
            wait_for(self.full.at[1 - k, self.chunk], self.swap_recv)

    hid = [RowGather(hall, i, hr.at[i], hsr, HID_STRAIGHT[i]) for i in range(N)]
    delta = [RowGather(dall, i, dr.at[i], dsr, DELTA_STRAIGHT[i]) for i in range(N)]

    class ColSum:
        def __init__(self, base, part, exact, received, summed, landed, result):
            self.base, self.part, self.exact, self.received = base, part, exact, received
            self.summed, self.landed, self.result = summed, landed, result

        def start(self, chunk):
            for s in reversed(range(S * chunk, S * chunk + S)):
                push(self.part.at[1 - yl, s], self.received.at[s], yr.at[self.base, s], yl_partner)

        def steps(self, chunk):
            for s in reversed(range(S * chunk, S * chunk + S)):
                self.step(s)

        def step(self, s):
            d = NEAR[s]
            wait_for(self.received.at[s], yr.at[self.base, s])
            total = self.exact[yl, s] + self.received[s].astype(F32)
            if d == 0:
                own[self.base] = total
            else:
                self.summed[s] = total.astype(BF16)
                push(self.summed.at[s], self.landed.at[d - 1], zr.at[self.base], z_dev(d))

        def finish(self):
            total = own[self.base]
            wait_for(self.landed, zr.at[self.base])
            for d in range(7):
                total += self.landed[d].astype(F32)
            self.result[...] = total.astype(BF16)

    sum_out = ColSum(0, po, pof, ro, so, zo, outv)
    sum_ing = ColSum(1, pi, pif, ri, si, zi, ingv)

    def out_tile(chunk, col):
        return nn(hall[:, chunk].reshape(2 * C, H), wd[:, pl.ds(col, T)])

    def ing_tile(chunk, col):
        left = dall[:, chunk].reshape(2 * C, 2 * H)
        return nt(left[:, :H], wg[pl.ds(col, T), :]) + nt(left[:, H:], wu[pl.ds(col, T), :])

    def col_sums(total, tile, chunk):
        slots = pl.ds(S * chunk, S)

        def both(col):
            value = tile(chunk, col).reshape(2, S, B, T)
            total.exact[:, slots, :, pl.ds(col, T)] = value
            total.part[:, slots, :, pl.ds(col, T)] = value.astype(BF16)

        tiles(F // T, both)
        total.start(chunk)

    def out_sums(chunk):
        hid[chunk].swapped()
        col_sums(sum_out, out_tile, chunk)

    def ing_sums(chunk):
        delta[chunk].swapped()
        col_sums(sum_ing, ing_tile, chunk)

    def tokens(ref, col):
        return ref[:, :, :, :, :, pl.ds(col, T)].reshape(16 * B, T)

    def gate_grad_tile(col):
        ggv[:, pl.ds(col, T)] = tn(xall[...].reshape(16 * B, F), tokens(dall, col)).astype(BF16)

    def up_grad_tile(col):
        up_col = pl.multiple_of(H + col, T)
        ugv[:, pl.ds(col, T)] = tn(xall[...].reshape(16 * B, F), tokens(dall, up_col)).astype(BF16)

    def down_grad_tile(col):
        dgv[pl.ds(col, T), :] = tn(tokens(hall, col), gall[...].reshape(16 * B, F)).astype(BF16)

    results = [
        pltpu.make_async_copy(src, dst, rsem.at[i]) for i, (src, dst) in enumerate(zip((outv, ingv, ggv, ugv, dgv), outs))
    ]

    local[0].wait()
    gat_x.send_pair()
    gat_x.send_own()
    local[1].wait()
    gat_g.send_pair()
    for i, (src, dst) in enumerate(((wg, wgs), (wu, wus), (wd, wds))):
        local[2 + i].wait()
        push(src, dst, wrecv.at[i], sibling)
    gat_g.send_own()
    gat_x.pair()
    gat_x.step(1)
    gat_g.pair()
    for i, dst in enumerate((wgs, wus, wds)):
        wait_for(dst, wrecv.at[i])
    gate_part(0)
    up_part(0)
    gat_x.step(2)
    gate_part(1)
    up_part(1)
    gat_g.step(1)
    gat_x.step(3)
    gate_part(2)
    up_part(2)
    gat_g.step(2)
    sum_gu[1].pair()
    sum_gu[0].pair()
    gat_x.step(4)
    gate_part(3)
    up_part(3)
    hidden_of(1)
    sum_gu[2].pair()
    hidden_grad(1)
    gat_g.step(3)
    hidden_grad(2)
    sum_gu[3].pair()
    hid[1].near()
    gat_g.step(4)
    hidden_of(2)
    hidden_of(3)
    hidden_grad(3)
    hid[1].far()
    hidden_of(0)
    sum_h[1].pair()
    sum_h[2].pair()
    hid[2].near()
    out_sums(1)
    hid[3].near()
    hid[3].far()
    deltas_of(1)
    sum_h[3].pair()
    out_sums(3)
    hid[0].near()
    hidden_grad(0)
    sum_out.step(3)
    sum_out.step(2)
    hid[2].far()
    out_sums(2)
    delta[1].near()
    hid[0].far()
    sum_out.step(7)
    deltas_of(3)
    sum_out.step(6)
    out_sums(0)
    delta[1].far()
    sum_h[0].pair()
    sum_out.step(5)
    ing_sums(1)
    deltas_of(2)
    sum_out.step(1)
    delta[3].near()
    sum_out.step(4)
    delta[3].far()
    ing_sums(3)
    deltas_of(0)
    sum_out.step(0)
    delta[2].near()
    sum_ing.step(3)
    sum_ing.step(2)
    delta[2].far()
    sum_ing.step(7)
    ing_sums(2)
    delta[0].near()
    sum_ing.step(6)
    tiles(H // T, down_grad_tile)
    results[4].start()
    delta[0].far()
    sum_ing.step(5)
    ing_sums(0)
    sum_ing.step(4)
    sum_out.finish()
    results[0].start()
    sum_ing.step(1)
    tiles(H // T, up_grad_tile)
    results[3].start()
    tiles(H // T, gate_grad_tile)
    results[2].start()
    sum_ing.step(0)
    sum_ing.finish()
    results[1].start()
    for copy in pending[-POOL:]:
        copy.wait_send()
    for copy in results:
        copy.wait()


def deliver(*refs):
    sources, results, held, sems = refs[:5], refs[5:10], refs[10:15], refs[15]
    pieces = [(i, pl.ds(row, 128)) for i in range(2, 5) for row in range(0, sources[i].shape[0], 128)]
    pieces += [(i, pl.ds(0, B)) for i in range(2)]
    loads = [pltpu.make_async_copy(sources[i].at[r], held[i].at[r], sems.at[0, n]) for n, (i, r) in enumerate(pieces)]
    stores = [pltpu.make_async_copy(held[i].at[r], results[i].at[r], sems.at[1, n]) for n, (i, r) in enumerate(pieces)]
    for load in loads:
        load.start()
    for load, store in zip(loads, stores):
        load.wait()
        store.start()
    for store in stores:
        store.wait()


def body(inputs, gate_weight, up_weight, down_weight, out_grad):
    dma = pltpu.SemaphoreType.DMA
    shapes = tuple(jax.ShapeDtypeStruct(shape, BF16) for shape in ((B, F), (B, F), (F, H), (F, H), (H, F)))
    bf = lambda *shape: pltpu.VMEM(shape, BF16)
    f32 = lambda *shape: pltpu.VMEM(shape, F32)
    results = pl.pallas_call(
        kernel,
        out_shape=shapes,
        in_specs=[pl.BlockSpec(memory_space=pl.ANY)] * 5,
        out_specs=(pl.BlockSpec(memory_space=pl.ANY),) * 5,
        scratch_shapes=[
            bf(2, 8, B, F), bf(2, 8, B, F), bf(8, B, F), bf(8, B, F),
            bf(F, H), bf(F, H), bf(H, F), bf(F, H), bf(F, H), bf(H, F),
            bf(N, 2, 4, R, 2 * H), bf(N, 2, 4, R, H), f32(N, 2, 4, R, 2 * H), f32(N, 2, 4, R, H),
            bf(N, 3, 2, R, 2 * H), f32(N, 2, R, 2 * H), bf(N, 2, R, 2 * H), bf(N, 2, R, 2 * H),
            bf(N, 3, 2, R, H), f32(N, 2, R, H), bf(N, 2, R, H), bf(N, 2, R, H),
            f32(N, 2, R, 2 * H), bf(2, N, 2, 4, R, H), bf(2, N, 2, 4, R, 2 * H),
            bf(2, 8, B, F), f32(2, 8, B, F), bf(8, B, F), bf(8, B, F), bf(7, B, F),
            bf(2, 8, B, F), f32(2, 8, B, F), bf(8, B, F), bf(8, B, F), bf(7, B, F),
            f32(2, B, F), bf(B, F), bf(B, F), bf(F, H), bf(F, H), bf(H, F),
            dma((5,)), dma((POOL,)), dma((3,)),
            dma((2, 2, 4)), dma, dma((2, 2, 4)), dma, dma((N,)), dma((N,)),
            dma((N, 2)), dma((N, 2)), dma((N, 2, 1, 2)), dma((N, 2, 1, 2)), dma((N,)), dma((N,)),
            dma((2, 8)), dma((2,)), dma((5,)),
        ],
        compiler_params=pltpu.CompilerParams(collective_id=0, has_side_effects=True, vmem_limit_bytes=60 << 20),
        name="ffn",
    )(inputs, gate_weight, up_weight, down_weight, out_grad)
    return pl.pallas_call(
        deliver,
        out_shape=shapes,
        in_specs=[pl.BlockSpec(memory_space=pl.ANY)] * 5,
        out_specs=(pl.BlockSpec(memory_space=pl.ANY),) * 5,
        scratch_shapes=[*[pltpu.VMEM(shape.shape, BF16) for shape in shapes], dma((2, 16))],
        name="deliver",
    )(*results)


def solution(mesh):
    return jax.shard_map(
        body,
        mesh=mesh,
        in_specs=(P("col", "row"), P("row", "col"), P("row", "col"), P("col", "row"), P("col", "row")),
        out_specs=(P("col", "row"), P("col", "row"), P("row", "col"), P("row", "col"), P("col", "row")),
        check_vma=False,
    )
```

```python
import jax
import jax.numpy as jnp
from jax import lax
from jax.experimental import pallas as pl
from jax.experimental.pallas import tpu as pltpu
from jax.sharding import PartitionSpec as P

MESH = pl.DeviceIdType.MESH
F32 = jnp.float32
BF16 = jnp.bfloat16
B = 64
F = 512
H = 768
T = 256
NEAR = (0, 1, 7, 2, 6, 3, 5, 4)
SLOT = tuple(NEAR.index(d) for d in range(8))
N = 4
S = 8 // N
C = S * B
R = C // 8
POOL = 24
HID_STRAIGHT = (False, False, False, True)
DELTA_STRAIGHT = (True, False, True, True)


def nn(left, right):
    return jnp.dot(left, right, preferred_element_type=F32)


def nt(left, right):
    return lax.dot_general(left, right, (((1,), (1,)), ((), ())), preferred_element_type=F32)


def tn(left, right):
    return lax.dot_general(left, right, (((0,), (0,)), ((), ())), preferred_element_type=F32)


def tiles(count, body):
    def step(i, carry):
        body(pl.multiple_of(i * T, T))
        return carry

    lax.fori_loop(0, count, step, 0)


class Ring:
    def __init__(self, far, src, dst, view, half, neighbour, sems, push, wait_for):
        self.far, self.src, self.dst, self.view, self.half = far, src, dst, view, half
        self.neighbour, self.sems, self.push, self.wait_for = neighbour, sems, push, wait_for

    def part(self, ref, dist, way):
        return self.half(ref, way) if dist == self.far else ref

    def send(self, lane, dist, way):
        src, dst = [self.part(ref, dist, way) for ref in (self.src(lane, dist - 1, way), self.dst(lane, dist, way))]
        self.push(src, dst, self.sems.at[way, lane, dist - 1], self.neighbour(way))

    def wait(self, lane, dist, way):
        self.wait_for(self.part(self.view(lane, dist, way), dist, way), self.sems.at[way, lane, dist - 1])


def kernel(
    x_hbm, wg_hbm, wu_hbm, wd_hbm, g_hbm,
    *refs,
):
    outs = refs[:5]
    (
        xall, gall, xsib, gsib, wg, wu, wd, wgs, wus, wds, pg, ph, pgf, phf,
        glanded, gtotal, ghalf, gother, hlanded, htotal, hhalf, hother, gu, hall, dall,
        po, pof, ro, so, zo, pi, pif, ri, si, zi, own, outv, ingv, ggv, ugv, dgv,
        lsem, pool, wrecv, xr, xpr, gr, gpr, xsr, gsr, rgr, rhr, hr, dr, hsr, dsr, yr, zr,
    ) = refs[5:]
    r = lax.axis_index("row")
    c = lax.axis_index("col")
    yh, x, k = r // 8, (r // 2) % 4, r % 2
    z, yl = c // 2, c % 2
    pending = []

    sibling = (yh * 8 + x * 2 + (1 - k), c)
    yl_partner = (r, z * 2 + (1 - yl))
    yh_partner = ((1 - yh) * 8 + x * 2 + k, c)

    def z_dev(d):
        return (r, lax.rem(z + d, 8) * 2 + yl)

    def z_next(way):
        return z_dev(1 if way == 0 else 7)

    def x_dev(d):
        return (yh * 8 + lax.rem(x + d, 4) * 2 + k, c)

    def x_next(way):
        return x_dev(1 if way == 0 else 3)

    def push(src, dst, recv, device):
        count = len(pending)
        if count >= POOL:
            pending[count - POOL].wait_send()
        copy = pltpu.make_async_remote_copy(
            src_ref=src, dst_ref=dst, send_sem=pool.at[count % POOL], recv_sem=recv,
            device_id=device, device_id_type=MESH,
        )
        copy.start()
        pending.append(copy)

    def wait_for(ref, recv):
        pltpu.make_async_remote_copy(
            src_ref=ref, dst_ref=ref, send_sem=pool.at[0], recv_sem=recv, device_id=sibling, device_id_type=MESH
        ).wait_recv()

    local = [
        pltpu.make_async_copy(src, dst, lsem.at[i])
        for i, (src, dst) in enumerate((
            (x_hbm, xall.at[yl, 0]), (g_hbm, gall.at[yl, 0]), (wg_hbm, wg), (wu_hbm, wu), (wd_hbm, wd),
        ))
    ]
    for copy in local:
        copy.start()
    barrier = pltpu.get_barrier_semaphore()
    peers = [sibling, yl_partner, yh_partner] + [x_dev(d) for d in range(1, 4)] + [z_dev(d) for d in range(1, 8)]
    for peer in peers:
        pl.semaphore_signal(barrier, inc=1, device_id=peer, device_id_type=MESH)
    pl.semaphore_wait(barrier, len(peers))

    def half_rows(ref, way):
        return ref.at[pl.ds(way * (B // 2), B // 2)]

    class Gather:
        def __init__(self, full, half, recv, pair_recv, swap_recv):
            def at(lane, dist, way):
                return full.at[yl if lane == 0 else 1 - yl, SLOT[(dist if way else 8 - dist) % 8]]

            self.full, self.half_tokens, self.pair_recv, self.swap_recv = full, half, pair_recv, swap_recv
            self.ring = Ring(4, at, at, at, half_rows, z_next, recv, push, wait_for)

        def send_pair(self):
            ref = self.full.at[yl, 0]
            push(ref, ref, self.pair_recv, yl_partner)

        def send_own(self):
            for way in (0, 1):
                self.ring.send(0, 1, way)

        def pair(self):
            ref = self.full.at[1 - yl, 0]
            wait_for(ref, self.pair_recv)
            for way in (0, 1):
                self.ring.send(1, 1, way)
            self.swap(0)

        def step(self, dist):
            for lane in (0, 1):
                for way in (0, 1):
                    self.ring.wait(lane, dist, way)
                    if dist < 4:
                        self.ring.send(lane, dist + 1, way)
            for d in sorted({dist, 8 - dist}):
                self.swap(SLOT[d])

        def swap(self, s):
            push(self.full.at[1 - k, s], self.half_tokens.at[s], self.swap_recv.at[s // S], sibling)

        def swapped(self, chunk):
            wait_for(self.half_tokens.at[pl.ds(S * chunk, S)], self.swap_recv.at[chunk])

    gat_x = Gather(xall, xsib, xr, xpr, xsr)
    gat_g = Gather(gall, gsib, gr, gpr, gsr)

    def chunk_of(ref, chunk):
        return ref[pl.ds(S * chunk, S)].reshape(C, F)

    def put_partial(value, part, exact, chunk, col):
        value = value.reshape(2, 4, R, T)
        exact[chunk, :, :, :, pl.ds(col, T)] = value
        part[chunk, :, :, :, pl.ds(col, T)] = value.astype(BF16)

    def half_sums(chunk, j):
        w, ws = ((wg, wgs), (wu, wus))[j]

        def tile(col):
            value = nn(chunk_of(xall.at[k], chunk), w[:, pl.ds(col, T)])
            value += nn(chunk_of(xsib, chunk), ws[:, pl.ds(col, T)])
            put_partial(value, pg, pgf, chunk, pl.multiple_of(j * H + col, T))

        tiles(H // T, tile)

    def hidden_grad_sums(chunk):
        gat_g.swapped(chunk)

        def tile(col):
            value = nt(chunk_of(gall.at[k], chunk), wd[pl.ds(col, T), :])
            value += nt(chunk_of(gsib, chunk), wds[pl.ds(col, T), :])
            put_partial(value, ph, phf, chunk, col)

        tiles(H // T, tile)

    class RowSum:
        def __init__(self, chunk, part, exact, landed, total, half, other, recv):
            self.part, self.exact, self.landed, self.total, self.half, self.other, self.recv = [
                ref.at[chunk] for ref in (part, exact, landed, total, half, other, recv)
            ]

        def send(self, first):
            cols = pl.ds(first, H)
            for d in (2, 1, 3):
                src = self.part.at[:, lax.rem(x + d, 4), :, cols]
                push(src, self.landed.at[d - 1, :, :, cols], self.recv.at[0], x_dev(d))

        def pair(self):
            wait_for(self.landed, self.recv.at[0])
            for lane in (0, 1):
                value = self.exact[lane, x]
                for d in range(3):
                    value += self.landed[d, lane].astype(F32)
                self.total[lane] = value
                self.half[lane] = value.astype(BF16)
            push(self.half, self.other, self.recv.at[1], yh_partner)

        def finish(self):
            wait_for(self.other, self.recv.at[1])

        def value(self, lane, col):
            return self.total[lane, :, pl.ds(col, T)] + self.other[lane, :, pl.ds(col, T)].astype(F32)

    sum_gu = [RowSum(i, pg, pgf, glanded, gtotal, ghalf, gother, rgr) for i in range(N)]
    sum_h = [RowSum(i, ph, phf, hlanded, htotal, hhalf, hother, rhr) for i in range(N)]

    def gate_part(chunk):
        gat_x.swapped(chunk)
        half_sums(chunk, 0)
        sum_gu[chunk].send(0)

    def up_part(chunk):
        half_sums(chunk, 1)
        sum_gu[chunk].send(H)

    def hidden_grad(chunk):
        hidden_grad_sums(chunk)
        sum_h[chunk].send(0)

    def hidden_of(chunk):
        sum_gu[chunk].finish()

        def tile(col):
            up_col = pl.multiple_of(H + col, T)
            for lane in (0, 1):
                gate, up = sum_gu[chunk].value(lane, col), sum_gu[chunk].value(lane, up_col)
                gu[chunk, lane, :, pl.ds(col, T)] = gate
                gu[chunk, lane, :, pl.ds(up_col, T)] = up
                hall[k, chunk, lane, x, :, pl.ds(col, T)] = (gate * jax.nn.sigmoid(gate) * up).astype(BF16)

        tiles(H // T, tile)
        hid[chunk].start()

    def deltas_of(chunk):
        sum_h[chunk].finish()

        def tile(col):
            up_col = pl.multiple_of(H + col, T)
            for lane in (0, 1):
                hidden_grad = sum_h[chunk].value(lane, col)
                gate, up = gu[chunk, lane, :, pl.ds(col, T)], gu[chunk, lane, :, pl.ds(up_col, T)]
                sig = jax.nn.sigmoid(gate)
                dall[k, chunk, lane, x, :, pl.ds(up_col, T)] = (hidden_grad * (gate * sig)).astype(BF16)
                dall[k, chunk, lane, x, :, pl.ds(col, T)] = (
                    hidden_grad * up * sig * (1.0 + gate * (1.0 - sig))
                ).astype(BF16)

        tiles(H // T, tile)
        delta[chunk].start()

    class RowGather:
        def __init__(self, full, chunk, recv, swap_recv, straight):
            self.full, self.chunk, self.straight = full, chunk, straight
            self.far_recv, self.swap_recv = recv.at[0, 0, 1], swap_recv.at[chunk]

            def src(lane, dist, way):
                return self.block(k, dist if way else 4 - dist)

            def dst(lane, dist, way):
                return src(lane, dist - 1, way)

            self.ring = Ring(2, src, dst, src, lambda ref, way: ref.at[way], x_next, recv, push, wait_for)

        def block(self, core, d):
            return self.full.at[core, self.chunk, :, lax.rem(x + d, 4)]

        def swap(self, d):
            ref = self.block(k, d)
            push(ref, ref, self.swap_recv, sibling)

        def start(self):
            for way in (0, 1):
                self.ring.send(0, 1, way)
            if self.straight:
                push(self.block(k, 0), self.block(k, 0), self.far_recv, x_dev(2))
            self.swap(0)

        def near(self):
            for way in (0, 1):
                self.ring.wait(0, 1, way)
                if not self.straight:
                    self.ring.send(0, 2, way)
                self.swap(1 if way else 3)

        def far(self):
            if self.straight:
                wait_for(self.block(k, 2), self.far_recv)
            else:
                for way in (0, 1):
                    self.ring.wait(0, 2, way)
            self.swap(2)

        def swapped(self):
            wait_for(self.full.at[1 - k, self.chunk], self.swap_recv)

    hid = [RowGather(hall, i, hr.at[i], hsr, HID_STRAIGHT[i]) for i in range(N)]
    delta = [RowGather(dall, i, dr.at[i], dsr, DELTA_STRAIGHT[i]) for i in range(N)]

    class ColSum:
        def __init__(self, base, part, exact, received, summed, landed, result):
            self.base, self.part, self.exact, self.received = base, part, exact, received
            self.summed, self.landed, self.result = summed, landed, result

        def start(self, chunk):
            for s in reversed(range(S * chunk, S * chunk + S)):
                push(self.part.at[1 - yl, s], self.received.at[s], yr.at[self.base, s], yl_partner)

        def steps(self, chunk):
            for s in reversed(range(S * chunk, S * chunk + S)):
                self.step(s)

        def step(self, s):
            d = NEAR[s]
            wait_for(self.received.at[s], yr.at[self.base, s])
            total = self.exact[yl, s] + self.received[s].astype(F32)
            if d == 0:
                own[self.base] = total
            else:
                self.summed[s] = total.astype(BF16)
                push(self.summed.at[s], self.landed.at[d - 1], zr.at[self.base], z_dev(d))

        def finish(self):
            total = own[self.base]
            wait_for(self.landed, zr.at[self.base])
            for d in range(7):
                total += self.landed[d].astype(F32)
            self.result[...] = total.astype(BF16)

    sum_out = ColSum(0, po, pof, ro, so, zo, outv)
    sum_ing = ColSum(1, pi, pif, ri, si, zi, ingv)

    def out_tile(chunk, col):
        return nn(hall[:, chunk].reshape(2 * C, H), wd[:, pl.ds(col, T)])

    def ing_tile(chunk, col):
        left = dall[:, chunk].reshape(2 * C, 2 * H)
        return nt(left[:, :H], wg[pl.ds(col, T), :]) + nt(left[:, H:], wu[pl.ds(col, T), :])

    def col_sums(total, tile, chunk):
        slots = pl.ds(S * chunk, S)

        def both(col):
            value = tile(chunk, col).reshape(2, S, B, T)
            total.exact[:, slots, :, pl.ds(col, T)] = value
            total.part[:, slots, :, pl.ds(col, T)] = value.astype(BF16)

        tiles(F // T, both)
        total.start(chunk)

    def out_sums(chunk):
        hid[chunk].swapped()
        col_sums(sum_out, out_tile, chunk)

    def ing_sums(chunk):
        delta[chunk].swapped()
        col_sums(sum_ing, ing_tile, chunk)

    def tokens(ref, col):
        return ref[:, :, :, :, :, pl.ds(col, T)].reshape(16 * B, T)

    def gate_grad_tile(col):
        ggv[:, pl.ds(col, T)] = tn(xall[...].reshape(16 * B, F), tokens(dall, col)).astype(BF16)

    def up_grad_tile(col):
        up_col = pl.multiple_of(H + col, T)
        ugv[:, pl.ds(col, T)] = tn(xall[...].reshape(16 * B, F), tokens(dall, up_col)).astype(BF16)

    def down_grad_tile(col):
        dgv[pl.ds(col, T), :] = tn(tokens(hall, col), gall[...].reshape(16 * B, F)).astype(BF16)

    results = [
        pltpu.make_async_copy(src, dst, lsem.at[i]) for i, (src, dst) in enumerate(zip((outv, ingv, ggv, ugv, dgv), outs))
    ]

    local[0].wait()
    gat_x.send_pair()
    gat_x.send_own()
    local[1].wait()
    gat_g.send_pair()
    for i, (src, dst) in enumerate(((wg, wgs), (wu, wus), (wd, wds))):
        local[2 + i].wait()
        push(src, dst, wrecv.at[i], sibling)
    gat_g.send_own()
    gat_x.pair()
    gat_x.step(1)
    gat_g.pair()
    for i, dst in enumerate((wgs, wus, wds)):
        wait_for(dst, wrecv.at[i])
    gate_part(0)
    up_part(0)
    gat_x.step(2)
    gate_part(1)
    up_part(1)
    gat_g.step(1)
    gat_x.step(3)
    gate_part(2)
    up_part(2)
    gat_g.step(2)
    sum_gu[1].pair()
    sum_gu[0].pair()
    gat_x.step(4)
    gate_part(3)
    up_part(3)
    hidden_of(1)
    sum_gu[2].pair()
    hidden_grad(1)
    gat_g.step(3)
    hidden_grad(2)
    sum_gu[3].pair()
    hid[1].near()
    gat_g.step(4)
    hidden_of(2)
    hidden_of(3)
    hidden_grad(3)
    hid[1].far()
    hidden_of(0)
    sum_h[1].pair()
    sum_h[2].pair()
    hid[2].near()
    out_sums(1)
    hid[3].near()
    hid[3].far()
    deltas_of(1)
    sum_h[3].pair()
    out_sums(3)
    hid[0].near()
    hidden_grad(0)
    sum_out.step(3)
    sum_out.step(2)
    hid[2].far()
    out_sums(2)
    delta[1].near()
    hid[0].far()
    sum_out.step(7)
    deltas_of(3)
    sum_out.step(6)
    out_sums(0)
    delta[1].far()
    sum_h[0].pair()
    sum_out.step(5)
    ing_sums(1)
    deltas_of(2)
    sum_out.step(1)
    delta[3].near()
    sum_out.step(4)
    delta[3].far()
    ing_sums(3)
    deltas_of(0)
    sum_out.step(0)
    delta[2].near()
    sum_ing.step(3)
    sum_ing.step(2)
    delta[2].far()
    sum_ing.step(7)
    ing_sums(2)
    delta[0].near()
    sum_ing.step(6)
    tiles(H // T, down_grad_tile)
    results[4].start()
    delta[0].far()
    sum_ing.step(5)
    ing_sums(0)
    sum_ing.step(4)
    sum_out.finish()
    results[0].start()
    sum_ing.step(1)
    tiles(H // T, up_grad_tile)
    results[3].start()
    tiles(H // T, gate_grad_tile)
    results[2].start()
    sum_ing.step(0)
    sum_ing.finish()
    results[1].start()
    for copy in pending[-POOL:]:
        copy.wait_send()
    for copy in results:
        copy.wait()


def deliver(*refs):
    sources, results, held, sems = refs[:5], refs[5:10], refs[10:15], refs[15]
    pieces = [(i, pl.ds(row, 128)) for i in range(2, 5) for row in range(0, sources[i].shape[0], 128)]
    pieces += [(i, pl.ds(0, B)) for i in range(2)]
    loads = [pltpu.make_async_copy(sources[i].at[r], held[i].at[r], sems.at[0, n]) for n, (i, r) in enumerate(pieces)]
    stores = [pltpu.make_async_copy(held[i].at[r], results[i].at[r], sems.at[1, n]) for n, (i, r) in enumerate(pieces)]
    for load in loads:
        load.start()
    for load, store in zip(loads, stores):
        load.wait()
        store.start()
    for store in stores:
        store.wait()


def body(inputs, gate_weight, up_weight, down_weight, out_grad):
    dma = pltpu.SemaphoreType.DMA
    shapes = tuple(jax.ShapeDtypeStruct(shape, BF16) for shape in ((B, F), (B, F), (F, H), (F, H), (H, F)))
    bf = lambda *shape: pltpu.VMEM(shape, BF16)
    f32 = lambda *shape: pltpu.VMEM(shape, F32)
    results = pl.pallas_call(
        kernel,
        out_shape=shapes,
        in_specs=[pl.BlockSpec(memory_space=pl.ANY)] * 5,
        out_specs=(pl.BlockSpec(memory_space=pl.ANY),) * 5,
        scratch_shapes=[
            bf(2, 8, B, F), bf(2, 8, B, F), bf(8, B, F), bf(8, B, F),
            bf(F, H), bf(F, H), bf(H, F), bf(F, H), bf(F, H), bf(H, F),
            bf(N, 2, 4, R, 2 * H), bf(N, 2, 4, R, H), f32(N, 2, 4, R, 2 * H), f32(N, 2, 4, R, H),
            bf(N, 3, 2, R, 2 * H), f32(N, 2, R, 2 * H), bf(N, 2, R, 2 * H), bf(N, 2, R, 2 * H),
            bf(N, 3, 2, R, H), f32(N, 2, R, H), bf(N, 2, R, H), bf(N, 2, R, H),
            f32(N, 2, R, 2 * H), bf(2, N, 2, 4, R, H), bf(2, N, 2, 4, R, 2 * H),
            bf(2, 8, B, F), f32(2, 8, B, F), bf(8, B, F), bf(8, B, F), bf(7, B, F),
            bf(2, 8, B, F), f32(2, 8, B, F), bf(8, B, F), bf(8, B, F), bf(7, B, F),
            f32(2, B, F), bf(B, F), bf(B, F), bf(F, H), bf(F, H), bf(H, F),
            dma((5,)), dma((POOL,)), dma((3,)),
            dma((2, 2, 4)), dma, dma((2, 2, 4)), dma, dma((N,)), dma((N,)),
            dma((N, 2)), dma((N, 2)), dma((N, 2, 1, 2)), dma((N, 2, 1, 2)), dma((N,)), dma((N,)),
            dma((2, 8)), dma((2,)),
        ],
        compiler_params=pltpu.CompilerParams(collective_id=0, has_side_effects=True, vmem_limit_bytes=60 << 20),
        name="ffn",
    )(inputs, gate_weight, up_weight, down_weight, out_grad)
    return pl.pallas_call(
        deliver,
        out_shape=shapes,
        in_specs=[pl.BlockSpec(memory_space=pl.ANY)] * 5,
        out_specs=(pl.BlockSpec(memory_space=pl.ANY),) * 5,
        scratch_shapes=[*[pltpu.VMEM(shape.shape, BF16) for shape in shapes], dma((2, 16))],
        name="deliver",
    )(*results)


def solution(mesh):
    return jax.shard_map(
        body,
        mesh=mesh,
        in_specs=(P("col", "row"), P("row", "col"), P("row", "col"), P("col", "row"), P("col", "row")),
        out_specs=(P("col", "row"), P("col", "row"), P("row", "col"), P("row", "col"), P("col", "row")),
        check_vma=False,
    )
```

```python
import jax
import jax.numpy as jnp
from jax import lax
from jax.experimental import pallas as pl
from jax.experimental.pallas import tpu as pltpu
from jax.sharding import PartitionSpec as P

MESH = pl.DeviceIdType.MESH
F32 = jnp.float32
BF16 = jnp.bfloat16
B = 64
F = 512
H = 768
T = 256
NEAR = (0, 1, 7, 2, 6, 3, 5, 4)
SLOT = tuple(NEAR.index(d) for d in range(8))
N = 4
S = 8 // N
C = S * B
R = C // 8
POOL = 24
HID_STRAIGHT = (False, False, False, True)
DELTA_STRAIGHT = (True, False, True, True)


def nn(left, right):
    return jnp.dot(left, right, preferred_element_type=F32)


def nt(left, right):
    return lax.dot_general(left, right, (((1,), (1,)), ((), ())), preferred_element_type=F32)


def tn(left, right):
    return lax.dot_general(left, right, (((0,), (0,)), ((), ())), preferred_element_type=F32)


def tiles(count, body):
    def step(i, carry):
        body(pl.multiple_of(i * T, T))
        return carry

    lax.fori_loop(0, count, step, 0)


class Ring:
    def __init__(self, far, src, dst, view, half, neighbour, sems, push, wait_for):
        self.far, self.src, self.dst, self.view, self.half = far, src, dst, view, half
        self.neighbour, self.sems, self.push, self.wait_for = neighbour, sems, push, wait_for

    def part(self, ref, dist, way):
        return self.half(ref, way) if dist == self.far else ref

    def send(self, lane, dist, way):
        src, dst = [self.part(ref, dist, way) for ref in (self.src(lane, dist - 1, way), self.dst(lane, dist, way))]
        self.push(src, dst, self.sems.at[way, lane, dist - 1], self.neighbour(way))

    def wait(self, lane, dist, way):
        self.wait_for(self.part(self.view(lane, dist, way), dist, way), self.sems.at[way, lane, dist - 1])


def kernel(
    x_hbm, wg_hbm, wu_hbm, wd_hbm, g_hbm,
    *refs,
):
    outs = refs[:5]
    (
        xall, gall, xsib, gsib, wg, wu, wd, wgs, wus, wds, pg, ph, pgf, phf,
        glanded, gtotal, ghalf, gother, hlanded, htotal, hhalf, hother, gu, hall, dall,
        po, pof, ro, so, zo, pi, pif, ri, si, zi, own, outv, ingv, ggv, ugv, dgv,
        lsem, pool, wrecv, xr, xpr, gr, gpr, xsr, gsr, rgr, rhr, hr, dr, hsr, dsr, yr, zr,
    ) = refs[5:]
    r = lax.axis_index("row")
    c = lax.axis_index("col")
    yh, x, k = r // 8, (r // 2) % 4, r % 2
    z, yl = c // 2, c % 2
    pending = []

    sibling = (yh * 8 + x * 2 + (1 - k), c)
    yl_partner = (r, z * 2 + (1 - yl))
    yh_partner = ((1 - yh) * 8 + x * 2 + k, c)

    def z_dev(d):
        return (r, lax.rem(z + d, 8) * 2 + yl)

    def z_next(way):
        return z_dev(1 if way == 0 else 7)

    def x_dev(d):
        return (yh * 8 + lax.rem(x + d, 4) * 2 + k, c)

    def x_next(way):
        return x_dev(1 if way == 0 else 3)

    def push(src, dst, recv, device):
        count = len(pending)
        if count >= POOL:
            pending[count - POOL].wait_send()
        copy = pltpu.make_async_remote_copy(
            src_ref=src, dst_ref=dst, send_sem=pool.at[count % POOL], recv_sem=recv,
            device_id=device, device_id_type=MESH,
        )
        copy.start()
        pending.append(copy)

    def wait_for(ref, recv):
        pltpu.make_async_remote_copy(
            src_ref=ref, dst_ref=ref, send_sem=pool.at[0], recv_sem=recv, device_id=sibling, device_id_type=MESH
        ).wait_recv()

    local = [
        pltpu.make_async_copy(src, dst, lsem.at[i])
        for i, (src, dst) in enumerate((
            (x_hbm, xall.at[yl, 0]), (g_hbm, gall.at[yl, 0]), (wg_hbm, wg), (wu_hbm, wu), (wd_hbm, wd),
        ))
    ]
    for copy in local:
        copy.start()
    barrier = pltpu.get_barrier_semaphore()
    peers = [sibling, yl_partner, yh_partner] + [x_dev(d) for d in range(1, 4)] + [z_dev(d) for d in range(1, 8)]
    for peer in peers:
        pl.semaphore_signal(barrier, inc=1, device_id=peer, device_id_type=MESH)
    pl.semaphore_wait(barrier, len(peers))

    def half_rows(ref, way):
        return ref.at[pl.ds(way * (B // 2), B // 2)]

    class Gather:
        def __init__(self, full, half, recv, pair_recv, swap_recv):
            def at(lane, dist, way):
                return full.at[yl if lane == 0 else 1 - yl, SLOT[(dist if way else 8 - dist) % 8]]

            self.full, self.half_tokens, self.pair_recv, self.swap_recv = full, half, pair_recv, swap_recv
            self.ring = Ring(4, at, at, at, half_rows, z_next, recv, push, wait_for)

        def send_pair(self):
            ref = self.full.at[yl, 0]
            push(ref, ref, self.pair_recv, yl_partner)

        def send_own(self):
            for way in (0, 1):
                self.ring.send(0, 1, way)

        def pair(self):
            ref = self.full.at[1 - yl, 0]
            wait_for(ref, self.pair_recv)
            for way in (0, 1):
                self.ring.send(1, 1, way)
            self.swap(0)

        def step(self, dist):
            for lane in (0, 1):
                for way in (0, 1):
                    self.ring.wait(lane, dist, way)
                    if dist < 4:
                        self.ring.send(lane, dist + 1, way)
            for d in sorted({dist, 8 - dist}):
                self.swap(SLOT[d])

        def swap(self, s):
            push(self.full.at[1 - k, s], self.half_tokens.at[s], self.swap_recv.at[s // S], sibling)

        def swapped(self, chunk):
            wait_for(self.half_tokens.at[pl.ds(S * chunk, S)], self.swap_recv.at[chunk])

    gat_x = Gather(xall, xsib, xr, xpr, xsr)
    gat_g = Gather(gall, gsib, gr, gpr, gsr)

    def chunk_of(ref, chunk):
        return ref[pl.ds(S * chunk, S)].reshape(C, F)

    def put_partial(value, part, exact, chunk, col):
        value = value.reshape(2, 4, R, T)
        exact[chunk, :, :, :, pl.ds(col, T)] = value
        part[chunk, :, :, :, pl.ds(col, T)] = value.astype(BF16)

    def half_sums(chunk, j):
        w, ws = ((wg, wgs), (wu, wus))[j]

        def tile(col):
            value = nn(chunk_of(xall.at[k], chunk), w[:, pl.ds(col, T)])
            value += nn(chunk_of(xsib, chunk), ws[:, pl.ds(col, T)])
            put_partial(value, pg, pgf, chunk, pl.multiple_of(j * H + col, T))

        tiles(H // T, tile)

    def hidden_grad_sums(chunk):
        gat_g.swapped(chunk)

        def tile(col):
            value = nt(chunk_of(gall.at[k], chunk), wd[pl.ds(col, T), :])
            value += nt(chunk_of(gsib, chunk), wds[pl.ds(col, T), :])
            put_partial(value, ph, phf, chunk, col)

        tiles(H // T, tile)

    class RowSum:
        def __init__(self, chunk, part, exact, landed, total, half, other, recv):
            self.part, self.exact, self.landed, self.total, self.half, self.other, self.recv = [
                ref.at[chunk] for ref in (part, exact, landed, total, half, other, recv)
            ]

        def send(self, first):
            cols = pl.ds(first, H)
            for d in (2, 1, 3):
                src = self.part.at[:, lax.rem(x + d, 4), :, cols]
                push(src, self.landed.at[d - 1, :, :, cols], self.recv.at[0], x_dev(d))

        def pair(self):
            wait_for(self.landed, self.recv.at[0])
            for lane in (0, 1):
                value = self.exact[lane, x]
                for d in range(3):
                    value += self.landed[d, lane].astype(F32)
                self.total[lane] = value
                self.half[lane] = value.astype(BF16)
            push(self.half, self.other, self.recv.at[1], yh_partner)

        def finish(self):
            wait_for(self.other, self.recv.at[1])

        def value(self, lane, col):
            return self.total[lane, :, pl.ds(col, T)] + self.other[lane, :, pl.ds(col, T)].astype(F32)

    sum_gu = [RowSum(i, pg, pgf, glanded, gtotal, ghalf, gother, rgr) for i in range(N)]
    sum_h = [RowSum(i, ph, phf, hlanded, htotal, hhalf, hother, rhr) for i in range(N)]

    def gate_part(chunk):
        gat_x.swapped(chunk)
        half_sums(chunk, 0)
        sum_gu[chunk].send(0)

    def up_part(chunk):
        half_sums(chunk, 1)
        sum_gu[chunk].send(H)

    def hidden_grad(chunk):
        hidden_grad_sums(chunk)
        sum_h[chunk].send(0)

    def hidden_of(chunk):
        sum_gu[chunk].finish()

        def tile(col):
            up_col = pl.multiple_of(H + col, T)
            for lane in (0, 1):
                gate, up = sum_gu[chunk].value(lane, col), sum_gu[chunk].value(lane, up_col)
                gu[chunk, lane, :, pl.ds(col, T)] = gate
                gu[chunk, lane, :, pl.ds(up_col, T)] = up
                hall[k, chunk, lane, x, :, pl.ds(col, T)] = (gate * jax.nn.sigmoid(gate) * up).astype(BF16)

        tiles(H // T, tile)
        hid[chunk].start()

    def deltas_of(chunk):
        sum_h[chunk].finish()

        def tile(col):
            up_col = pl.multiple_of(H + col, T)
            for lane in (0, 1):
                hidden_grad = sum_h[chunk].value(lane, col)
                gate, up = gu[chunk, lane, :, pl.ds(col, T)], gu[chunk, lane, :, pl.ds(up_col, T)]
                sig = jax.nn.sigmoid(gate)
                dall[k, chunk, lane, x, :, pl.ds(up_col, T)] = (hidden_grad * (gate * sig)).astype(BF16)
                dall[k, chunk, lane, x, :, pl.ds(col, T)] = (
                    hidden_grad * up * sig * (1.0 + gate * (1.0 - sig))
                ).astype(BF16)

        tiles(H // T, tile)
        delta[chunk].start()

    class RowGather:
        def __init__(self, full, chunk, recv, swap_recv, straight):
            self.full, self.chunk, self.straight = full, chunk, straight
            self.far_recv, self.swap_recv = recv.at[0, 0, 1], swap_recv.at[chunk]

            def src(lane, dist, way):
                return self.block(k, dist if way else 4 - dist)

            def dst(lane, dist, way):
                return src(lane, dist - 1, way)

            self.ring = Ring(2, src, dst, src, lambda ref, way: ref.at[way], x_next, recv, push, wait_for)

        def block(self, core, d):
            return self.full.at[core, self.chunk, :, lax.rem(x + d, 4)]

        def swap(self, d):
            ref = self.block(k, d)
            push(ref, ref, self.swap_recv, sibling)

        def start(self):
            for way in (0, 1):
                self.ring.send(0, 1, way)
            if self.straight:
                push(self.block(k, 0), self.block(k, 0), self.far_recv, x_dev(2))
            self.swap(0)

        def near(self):
            for way in (0, 1):
                self.ring.wait(0, 1, way)
                if not self.straight:
                    self.ring.send(0, 2, way)
                self.swap(1 if way else 3)

        def far(self):
            if self.straight:
                wait_for(self.block(k, 2), self.far_recv)
            else:
                for way in (0, 1):
                    self.ring.wait(0, 2, way)
            self.swap(2)

        def swapped(self):
            wait_for(self.full.at[1 - k, self.chunk], self.swap_recv)

    hid = [RowGather(hall, i, hr.at[i], hsr, HID_STRAIGHT[i]) for i in range(N)]
    delta = [RowGather(dall, i, dr.at[i], dsr, DELTA_STRAIGHT[i]) for i in range(N)]

    class ColSum:
        def __init__(self, base, part, exact, received, summed, landed, result):
            self.base, self.part, self.exact, self.received = base, part, exact, received
            self.summed, self.landed, self.result = summed, landed, result

        def start(self, chunk):
            for s in reversed(range(S * chunk, S * chunk + S)):
                push(self.part.at[1 - yl, s], self.received.at[s], yr.at[self.base, s], yl_partner)

        def steps(self, chunk):
            for s in reversed(range(S * chunk, S * chunk + S)):
                self.step(s)

        def step(self, s):
            d = NEAR[s]
            wait_for(self.received.at[s], yr.at[self.base, s])
            total = self.exact[yl, s] + self.received[s].astype(F32)
            if d == 0:
                own[self.base] = total
            else:
                self.summed[s] = total.astype(BF16)
                push(self.summed.at[s], self.landed.at[d - 1], zr.at[self.base], z_dev(d))

        def finish(self):
            total = own[self.base]
            wait_for(self.landed, zr.at[self.base])
            for d in range(7):
                total += self.landed[d].astype(F32)
            self.result[...] = total.astype(BF16)

    sum_out = ColSum(0, po, pof, ro, so, zo, outv)
    sum_ing = ColSum(1, pi, pif, ri, si, zi, ingv)

    def out_tile(chunk, col):
        return nn(hall[:, chunk].reshape(2 * C, H), wd[:, pl.ds(col, T)])

    def ing_tile(chunk, col):
        left = dall[:, chunk].reshape(2 * C, 2 * H)
        return nt(left[:, :H], wg[pl.ds(col, T), :]) + nt(left[:, H:], wu[pl.ds(col, T), :])

    def col_sums(total, tile, chunk):
        slots = pl.ds(S * chunk, S)

        def both(col):
            value = tile(chunk, col).reshape(2, S, B, T)
            total.exact[:, slots, :, pl.ds(col, T)] = value
            total.part[:, slots, :, pl.ds(col, T)] = value.astype(BF16)

        tiles(F // T, both)
        total.start(chunk)

    def out_sums(chunk):
        hid[chunk].swapped()
        col_sums(sum_out, out_tile, chunk)

    def ing_sums(chunk):
        delta[chunk].swapped()
        col_sums(sum_ing, ing_tile, chunk)

    def tokens(ref, col):
        return ref[:, :, :, :, :, pl.ds(col, T)].reshape(16 * B, T)

    def gate_grad_tile(col):
        ggv[:, pl.ds(col, T)] = tn(xall[...].reshape(16 * B, F), tokens(dall, col)).astype(BF16)

    def up_grad_tile(col):
        up_col = pl.multiple_of(H + col, T)
        ugv[:, pl.ds(col, T)] = tn(xall[...].reshape(16 * B, F), tokens(dall, up_col)).astype(BF16)

    def down_grad_tile(col):
        dgv[pl.ds(col, T), :] = tn(tokens(hall, col), gall[...].reshape(16 * B, F)).astype(BF16)

    results = [
        pltpu.make_async_copy(src, dst, lsem.at[i]) for i, (src, dst) in enumerate(zip((outv, ingv, ggv, ugv, dgv), outs))
    ]

    local[0].wait()
    gat_x.send_pair()
    gat_x.send_own()
    local[1].wait()
    gat_g.send_pair()
    for i, (src, dst) in enumerate(((wg, wgs), (wu, wus), (wd, wds))):
        local[2 + i].wait()
        push(src, dst, wrecv.at[i], sibling)
    gat_g.send_own()
    gat_x.pair()
    gat_x.step(1)
    gat_g.pair()
    for i, dst in enumerate((wgs, wus, wds)):
        wait_for(dst, wrecv.at[i])
    gate_part(0)
    up_part(0)
    gat_x.step(2)
    gate_part(1)
    up_part(1)
    gat_g.step(1)
    gat_x.step(3)
    gate_part(2)
    up_part(2)
    gat_g.step(2)
    sum_gu[1].pair()
    sum_gu[0].pair()
    gat_x.step(4)
    gate_part(3)
    up_part(3)
    hidden_of(1)
    sum_gu[2].pair()
    hidden_grad(1)
    gat_g.step(3)
    hidden_grad(2)
    sum_gu[3].pair()
    hid[1].near()
    gat_g.step(4)
    hidden_of(2)
    hidden_of(3)
    hidden_grad(3)
    sum_h[2].pair()
    hid[1].far()
    hidden_of(0)
    sum_h[1].pair()
    hid[2].near()
    out_sums(1)
    hid[3].near()
    hid[3].far()
    deltas_of(1)
    sum_h[3].pair()
    out_sums(3)
    hid[0].near()
    hidden_grad(0)
    sum_out.step(3)
    sum_out.step(2)
    hid[2].far()
    out_sums(2)
    delta[1].near()
    hid[0].far()
    sum_out.step(7)
    deltas_of(3)
    sum_out.step(6)
    out_sums(0)
    delta[1].far()
    sum_h[0].pair()
    sum_out.step(5)
    ing_sums(1)
    deltas_of(2)
    sum_out.step(1)
    delta[3].near()
    sum_out.step(4)
    delta[3].far()
    ing_sums(3)
    deltas_of(0)
    sum_out.step(0)
    delta[2].near()
    sum_ing.step(3)
    sum_ing.step(2)
    delta[2].far()
    sum_ing.step(7)
    ing_sums(2)
    delta[0].near()
    sum_ing.step(6)
    tiles(H // T, down_grad_tile)
    results[4].start()
    delta[0].far()
    sum_ing.step(5)
    ing_sums(0)
    sum_ing.step(4)
    sum_out.finish()
    results[0].start()
    tiles(H // T, up_grad_tile)
    results[3].start()
    sum_ing.step(1)
    tiles(H // T, gate_grad_tile)
    results[2].start()
    sum_ing.step(0)
    sum_ing.finish()
    results[1].start()
    for copy in pending[-POOL:]:
        copy.wait_send()
    for copy in results:
        copy.wait()


def deliver(*refs):
    sources, results, held, sems = refs[:5], refs[5:10], refs[10:15], refs[15]
    pieces = [(i, pl.ds(row, 128)) for i in range(2, 5) for row in range(0, sources[i].shape[0], 128)]
    pieces += [(i, pl.ds(0, B)) for i in range(2)]
    loads = [pltpu.make_async_copy(sources[i].at[r], held[i].at[r], sems.at[0, n]) for n, (i, r) in enumerate(pieces)]
    stores = [pltpu.make_async_copy(held[i].at[r], results[i].at[r], sems.at[1, n]) for n, (i, r) in enumerate(pieces)]
    for load in loads:
        load.start()
    for load, store in zip(loads, stores):
        load.wait()
        store.start()
    for store in stores:
        store.wait()


def body(inputs, gate_weight, up_weight, down_weight, out_grad):
    dma = pltpu.SemaphoreType.DMA
    shapes = tuple(jax.ShapeDtypeStruct(shape, BF16) for shape in ((B, F), (B, F), (F, H), (F, H), (H, F)))
    bf = lambda *shape: pltpu.VMEM(shape, BF16)
    f32 = lambda *shape: pltpu.VMEM(shape, F32)
    results = pl.pallas_call(
        kernel,
        out_shape=shapes,
        in_specs=[pl.BlockSpec(memory_space=pl.ANY)] * 5,
        out_specs=(pl.BlockSpec(memory_space=pl.ANY),) * 5,
        scratch_shapes=[
            bf(2, 8, B, F), bf(2, 8, B, F), bf(8, B, F), bf(8, B, F),
            bf(F, H), bf(F, H), bf(H, F), bf(F, H), bf(F, H), bf(H, F),
            bf(N, 2, 4, R, 2 * H), bf(N, 2, 4, R, H), f32(N, 2, 4, R, 2 * H), f32(N, 2, 4, R, H),
            bf(N, 3, 2, R, 2 * H), f32(N, 2, R, 2 * H), bf(N, 2, R, 2 * H), bf(N, 2, R, 2 * H),
            bf(N, 3, 2, R, H), f32(N, 2, R, H), bf(N, 2, R, H), bf(N, 2, R, H),
            f32(N, 2, R, 2 * H), bf(2, N, 2, 4, R, H), bf(2, N, 2, 4, R, 2 * H),
            bf(2, 8, B, F), f32(2, 8, B, F), bf(8, B, F), bf(8, B, F), bf(7, B, F),
            bf(2, 8, B, F), f32(2, 8, B, F), bf(8, B, F), bf(8, B, F), bf(7, B, F),
            f32(2, B, F), bf(B, F), bf(B, F), bf(F, H), bf(F, H), bf(H, F),
            dma((5,)), dma((POOL,)), dma((3,)),
            dma((2, 2, 4)), dma, dma((2, 2, 4)), dma, dma((N,)), dma((N,)),
            dma((N, 2)), dma((N, 2)), dma((N, 2, 1, 2)), dma((N, 2, 1, 2)), dma((N,)), dma((N,)),
            dma((2, 8)), dma((2,)),
        ],
        compiler_params=pltpu.CompilerParams(collective_id=0, has_side_effects=True, vmem_limit_bytes=60 << 20),
        name="ffn",
    )(inputs, gate_weight, up_weight, down_weight, out_grad)
    return pl.pallas_call(
        deliver,
        out_shape=shapes,
        in_specs=[pl.BlockSpec(memory_space=pl.ANY)] * 5,
        out_specs=(pl.BlockSpec(memory_space=pl.ANY),) * 5,
        scratch_shapes=[*[pltpu.VMEM(shape.shape, BF16) for shape in shapes], dma((2, 16))],
        name="deliver",
    )(*results)


def solution(mesh):
    return jax.shard_map(
        body,
        mesh=mesh,
        in_specs=(P("col", "row"), P("row", "col"), P("row", "col"), P("col", "row"), P("col", "row")),
        out_specs=(P("col", "row"), P("col", "row"), P("row", "col"), P("row", "col"), P("col", "row")),
        check_vma=False,
    )
```
